32 devices in a mesh: seq: 4 (over y, core), exp: 8 (over z, x).
Axes of the slice: x: 2, y: 2, z: 4, core: 2. Of those that a mesh axis runs over, the one named last changes fastest.
Arguments:
- x_act: bfloat16 [8, 512, 4096], P('exp', 'seq'), may hold values from -6 to 6
- dt_low: bfloat16 [8, 512, 256], P('exp', 'seq'), may hold values from -6 to 6
- b_c: float32 [8, 512, 32], P('exp', 'seq'), may hold values from -6 to 6
- w_dt: bfloat16 [256, 4096], replicated, may hold values from -0.375 to 0.375
- dt_bias: float32 [4096], replicated, may hold values from -6 to -1
- a_log: float32 [16, 4096], replicated, may hold values from -1 to 2
- d_skip: float32 [4096], replicated, may hold values from 0.5 to 1.5
- w_router: bfloat16 [4, 4096], replicated, may hold values from -0.09375 to 0.09375
- expert_ids: int32 [8, 512, 2], P('exp', 'seq'), may hold values from 0 to 3, all different within a row; in each aligned block of 128 rows (0 to 127, 128 to 255, ..., all dimensions but the last counted through in order) at most 80 rows name the same one
- w_up: bfloat16 [8, 4096, 640], P('exp', 'seq'), may hold values from -0.09375 to 0.09375
- w_down: bfloat16 [8, 640, 4096], P('exp', None, 'seq'), may hold values from -0.15625 to 0.15625
Outputs:
- layer_out: bfloat16 [8, 512, 4096], P('exp', 'seq')
The draws below stay inside these ranges and needn't reach their ends.
Inputs may be any that keep to these rules, and one draw needn't show every extreme that they name: `expert_ids`: within the 128 tokens of one device (an aligned block), no expert is chosen by more than 80 tokens, and in some blocks one expert is chosen by exactly 80; a token's two experts differ.
All inputs are finite; a program needn't handle non-finite values.
Results may differ from the reference program's by a relative error of at most 0.011.
Values may be sent and summed in bfloat16 or wider, within the bound.
A program may use at most 128 MiB of HBM per device.

```python
import math
import jax
import jax.numpy as jnp
import numpy as np
from jax import lax

WIDTH = 4096
RANK = 256
NS = 16
EH = 640
TOK = 128
RECORDS = 8
LENGTH = 512
EXPERTS = 4
CAP = 80
N_EXP = 8


def block_levels(stream_key, extent, split, least, top_value):
    def one(dim, shards_of):
        steps = jax.random.uniform(jax.random.fold_in(jax.random.fold_in(stream_key, 6), dim), (shards_of,), jnp.float32, least / len(split), top_value / len(split))
        return jnp.repeat(jnp.exp(steps), extent[dim] // shards_of).reshape((-1,) + (1,) * (len(extent) - dim - 1))

    factor_of = one(*split[0])
    for cut in split[1:]:
        factor_of = factor_of * one(*cut)
    return factor_of


def deal_out(stream_key, own, number, rows, amount, top, bound, slope):
    sequence = jax.random.permutation(stream_key, amount)
    heavy_load, ordinary = load_shares(amount, rows * top, bound, slope, True), load_shares(amount, rows * top, bound, slope, False)
    places = jnp.arange(amount)

    def named(tallies, rotation):
        used = int((tallies > 0).sum())
        fixed = max(1, used // 4)
        passed = fixed + (places - fixed + rotation * (used - fixed)) % max(1, amount - fixed)
        return jnp.zeros((amount,), jnp.int32).at[sequence[jnp.where(places < fixed, places, passed)]].set(jnp.asarray(tallies, jnp.int32))

    tallies = jnp.where(number % 4 == 0, named(heavy_load, number // 4), named(ordinary, number - number // 4 - 1))
    mixed = jax.random.permutation(jax.random.fold_in(own, 3), amount)
    giver, receiver = mixed[0:amount // 2 * 2:2], mixed[1:amount // 2 * 2:2]
    room = jnp.minimum(tallies[giver] - 1, bound - tallies[receiver]) // 2
    room = jnp.where((giver == sequence[0]) | (receiver == sequence[0]) | (tallies[receiver] == 0), 0, jnp.maximum(room, 0))
    passed = jax.random.randint(jax.random.fold_in(own, 4), (amount // 2,), 0, 1 << 20) % (room + 1)
    tallies = tallies.at[giver].add(-passed).at[receiver].add(passed)
    labels = jnp.searchsorted(jnp.cumsum(tallies), jnp.arange(rows * top), side="right").astype(jnp.int32)
    grid = labels.reshape(top, rows).T
    grid = grid[jax.random.permutation(jax.random.fold_in(own, 1), rows)]
    rotation = jax.random.randint(jax.random.fold_in(own, 2), (rows, 1), 0, top)
    return jnp.take_along_axis(grid, (jnp.arange(top)[None, :] + rotation) % top, axis=1)


def load_shares(number_of, total, bound, skew, full):
    portions = [(1 << 20) // math.isqrt(grade ** skew) + 1 for grade in range(1, number_of + 1)]
    largest = bound if full else min(bound, max(-(-total // number_of), total * portions[0] // sum(portions)))
    least = 1 if total - largest >= number_of - 1 else 0
    counts, rest = [largest] + [least] * (number_of - 1), total - largest - least * (number_of - 1)
    while rest > 0:
        movable = [i for i in range(1, number_of) if counts[i] < largest] or [i for i in range(1, number_of) if counts[i] < bound]
        mass, budget = sum([portions[i] for i in movable]), rest
        for i in movable:
            more = min(bound - counts[i], max(1, budget * portions[i] // mass), rest)
            counts[i] = counts[i] + more
            rest = rest - more
    return np.array(counts)


def bell_draw(stream_key, dims, scale, bound, pieces=(), kind=jnp.bfloat16):
    gain = block_levels(stream_key, dims, pieces, -0.22, 0.18) if pieces else 1.0
    drawn = jax.random.normal(stream_key, dims, jnp.float32) * scale * gain
    return jnp.minimum(jnp.maximum(drawn, -bound), bound).astype(kind)


def setup_inputs(seed: int = 0) -> dict:
    key_of = jax.random.split(jax.random.key(seed), 12)
    x_act = bell_draw(key_of[0], (RECORDS, LENGTH, WIDTH), 1.0, 6.0, ((0, 8), (1, 4)))
    dt_low = bell_draw(key_of[1], (RECORDS, LENGTH, RANK), 1.0, 6.0, ((0, 8), (1, 4)))
    b_c = bell_draw(key_of[2], (RECORDS, LENGTH, 2 * NS), 1.0, 6.0, ((0, 8), (1, 4)), jnp.float32)
    w_dt = bell_draw(key_of[3], (RANK, WIDTH), RANK ** -0.5, 0.375)
    dt_bias = jnp.clip(jax.random.uniform(key_of[4], (WIDTH,), jnp.float32, -6.0, -1.0), -6.0, -1.0)
    a_log = jnp.clip(jax.random.uniform(key_of[5], (NS, WIDTH), jnp.float32, -1.0, 2.0), -1.0, 2.0)
    d_skip = jnp.clip(jax.random.uniform(key_of[6], (WIDTH,), jnp.float32, 0.5, 1.5), 0.5, 1.5)
    w_router = bell_draw(key_of[7], (EXPERTS, WIDTH), WIDTH ** -0.5, 0.09375)
    expert_ids_keys = jax.random.split(jax.random.fold_in(key_of[8], 1), RECORDS * LENGTH // TOK)
    expert_ids_turns = jax.random.permutation(jax.random.fold_in(key_of[8], 3), RECORDS * LENGTH // TOK)
    expert_ids = jax.vmap(lambda own, number: deal_out(jax.random.fold_in(key_of[8], 2), own, number, TOK, EXPERTS, 2, CAP, 2))(expert_ids_keys, expert_ids_turns).reshape((RECORDS, LENGTH, 2))
    w_up = bell_draw(key_of[9], (N_EXP, WIDTH, EH), WIDTH ** -0.5, 0.09375, ((0, 8), (1, 4)))
    w_down = bell_draw(key_of[10], (N_EXP, EH, WIDTH), (2 * EH) ** -0.5, 0.15625, ((0, 8), (2, 4)))
    return {"x_act": x_act, "dt_low": dt_low, "b_c": b_c, "w_dt": w_dt, "dt_bias": dt_bias, "a_log": a_log, "d_skip": d_skip, "w_router": w_router, "expert_ids": expert_ids, "w_up": w_up, "w_down": w_down}


def reference(x_act, dt_low, b_c, w_dt, dt_bias, a_log, d_skip, w_router, expert_ids, w_up, w_down):
    records, length, channels = x_act.shape
    low_rank = dt_low.shape[2]
    nstate = a_log.shape[0]
    pre = jnp.dot(dt_low.reshape(-1, low_rank), w_dt, preferred_element_type=jnp.float32)
    delta = jax.nn.softplus(pre.reshape(records, length, channels) + dt_bias)
    a_neg = -jnp.exp(a_log)
    xfloat = x_act.astype(jnp.float32)
    b_in = b_c[:, :, :nstate]
    c_out = b_c[:, :, nstate:]

    def advance(state, inputs):
        rate, driven, b_row, c_row = inputs
        state = jnp.exp(a_neg[None] * rate[:, None, :]) * state + driven[:, None, :] * b_row[:, :, None]
        return state, jnp.sum(c_row[:, :, None] * state, axis=1)

    start = jnp.zeros((records, nstate, channels), jnp.float32)
    _, outputs = lax.scan(advance, start, (jnp.swapaxes(delta, 0, 1), jnp.swapaxes(delta * xfloat, 0, 1), jnp.swapaxes(b_in, 0, 1), jnp.swapaxes(c_out, 0, 1)))
    scanned = jnp.swapaxes(outputs, 0, 1)
    mixer = (scanned + d_skip * xfloat).astype(jnp.bfloat16)

    rows_all = mixer.reshape(-1, channels)
    logits = jnp.dot(rows_all, w_router.T, preferred_element_type=jnp.float32)
    picks = expert_ids.reshape(-1, 2)
    chosen = jnp.take_along_axis(logits, picks, axis=1)
    first = jax.nn.sigmoid(chosen[:, 0] - chosen[:, 1])
    second = 1.0 - first
    blocks = rows_all.shape[0] // TOK
    pair_expert = picks.reshape(blocks, 2 * TOK)
    onehot = (pair_expert[:, :, None] == jnp.arange(EXPERTS, dtype=jnp.int32)[None, None, :]).astype(jnp.int32)
    position = jnp.sum(onehot * jnp.cumsum(onehot, axis=1), axis=2) - 1
    block_ids = jnp.broadcast_to(jnp.arange(blocks, dtype=jnp.int32)[:, None], (blocks, 2 * TOK))
    token_rows = block_ids * TOK + (jnp.arange(2 * TOK, dtype=jnp.int32) // 2)[None, :]
    table = jnp.zeros((blocks, EXPERTS, CAP), jnp.int32).at[block_ids, pair_expert, position].set(token_rows)

    def one_expert(index):
        rows = rows_all[table[:, index, :].reshape(-1)]
        total = jnp.zeros((rows.shape[0], channels), jnp.float32)
        for half in range(2):
            owner = 2 * index + half
            hidden = jax.nn.silu(jnp.dot(rows, w_up[owner], preferred_element_type=jnp.float32)).astype(jnp.bfloat16)
            partial_out = lax.optimization_barrier(jnp.dot(hidden, w_down[owner], preferred_element_type=jnp.float32).astype(jnp.bfloat16))
            total = total + partial_out.astype(jnp.float32)
        return total.astype(jnp.bfloat16)

    stacked = lax.map(one_expert, jnp.arange(EXPERTS, dtype=jnp.int32))
    flat_slot = block_ids * CAP + position
    picked = stacked[pair_expert.reshape(-1), flat_slot.reshape(-1)].reshape(-1, 2, channels).astype(jnp.float32)
    routed = first[:, None] * picked[:, 0] + second[:, None] * picked[:, 1]
    result = (rows_all.astype(jnp.float32) + routed).astype(jnp.bfloat16)
    return result.reshape(records, length, channels)
```

```python
import functools
import math

import jax
import jax.numpy as jnp
from jax import lax
from jax.experimental import pallas as pl
from jax.experimental.pallas import tpu as pltpu
from jax.sharding import PartitionSpec as P

LANES = 128
LOG2E = 1.0 / math.log(2.0)


def fold(rows):
    sub = lax.broadcasted_iota(jnp.int32, rows[0].shape, 0)
    for bit in (1, 2, 4):
        low = (sub & bit) == 0
        rows = [
            jnp.where(low, a, b) + pltpu.roll(jnp.where(low, b, a), 8 - bit, 0)
            for a, b in zip(rows[0::2], rows[1::2])
        ]
    return rows[0]


def fold_states(value):
    parts = [value[k : k + 8] for k in range(0, value.shape[0], 8)]
    return functools.reduce(jnp.add, parts)


def scan_kernel(
    x_ref, dt_ref, wdt_ref, bias_ref, alog_ref, b_ref, c_ref, y_ref, cum_ref, end_ref, delta_s, driven_s
):
    tokens, channels = x_ref.shape
    tiles = channels // LANES
    v = jnp.dot(dt_ref[...], wdt_ref[...], preferred_element_type=jnp.float32) + bias_ref[...]
    delta = jnp.maximum(v, 0.0) + jnp.log1p(jnp.exp(-jnp.abs(v)))
    delta_s[...] = delta
    driven_s[...] = delta * x_ref[...].astype(jnp.float32)
    rates = [
        -jnp.exp(alog_ref[:, j * LANES : (j + 1) * LANES]) * LOG2E for j in range(tiles)
    ]

    def body(group, carry):
        states, sums = list(carry[0]), list(carry[1])
        base = pl.multiple_of(group * 8, 8)
        partial = [[] for _ in range(tiles)]
        cums = [[] for _ in range(tiles)]
        delta8 = delta_s[pl.ds(base, 8), :]
        driven8 = driven_s[pl.ds(base, 8), :]
        for i in range(8):
            bt = b_ref[base + i]
            ct = c_ref[base + i]
            for j in range(tiles):
                cols = slice(j * LANES, (j + 1) * LANES)
                d = delta8[i : i + 1, cols]
                u = driven8[i : i + 1, cols]
                states[j] = jnp.exp2(rates[j] * d) * states[j] + u * bt
                partial[j].append(fold_states(ct * states[j]))
                sums[j] = sums[j] + d
                cums[j].append(sums[j])
        for j in range(tiles):
            cols = slice(j * LANES, (j + 1) * LANES)
            y_ref[pl.ds(base, 8), cols] = fold(partial[j])
            cum_ref[pl.ds(base, 8), cols] = jnp.concatenate(cums[j], axis=0)
        return tuple(states), tuple(sums)

    nstate = alog_ref.shape[0]
    init = (
        tuple(jnp.zeros((nstate, LANES), jnp.float32) for _ in range(tiles)),
        tuple(jnp.zeros((1, LANES), jnp.float32) for _ in range(tiles)),
    )
    states, _ = lax.fori_loop(0, tokens // 8, body, init)
    for j in range(tiles):
        end_ref[:, j * LANES : (j + 1) * LANES] = states[j]


def mix_kernel(
    x_ref, y_ref, cum_ref, alog_ref, start_ref, c_ref, skip_ref, pack_ref, mixer_ref, packed_ref, y_s
):
    tokens, channels = x_ref.shape
    tiles = channels // LANES
    rates = [
        -jnp.exp(alog_ref[:, j * LANES : (j + 1) * LANES]) * LOG2E for j in range(tiles)
    ]
    starts = [start_ref[:, j * LANES : (j + 1) * LANES] for j in range(tiles)]

    def body(group, carry):
        base = pl.multiple_of(group * 8, 8)
        partial = [[] for _ in range(tiles)]
        cum8 = cum_ref[pl.ds(base, 8), :]
        for i in range(8):
            ct = c_ref[base + i]
            for j in range(tiles):
                cols = slice(j * LANES, (j + 1) * LANES)
                d = cum8[i : i + 1, cols]
                partial[j].append(fold_states(ct * (jnp.exp2(rates[j] * d) * starts[j])))
        for j in range(tiles):
            y_s[pl.ds(base, 8), j * LANES : (j + 1) * LANES] = fold(partial[j])
        return carry

    lax.fori_loop(0, tokens // 8, body, 0)
    mixer = (y_s[...] + y_ref[...] + skip_ref[...] * x_ref[...].astype(jnp.float32)).astype(
        jnp.bfloat16
    )
    mixer_ref[...] = mixer
    packed_ref[...] = jnp.dot(pack_ref[...], mixer, preferred_element_type=jnp.float32).astype(
        jnp.bfloat16
    )


def final_kernel(mixer_ref, back_ref, one_ref, two_ref, w_ref, out_ref):
    back = back_ref[...]
    a = jnp.dot(one_ref[...], back, preferred_element_type=jnp.float32)
    b = jnp.dot(two_ref[...], back, preferred_element_type=jnp.float32)
    first = w_ref[:, 0:1]
    second = w_ref[:, 1:2]
    out_ref[...] = (mixer_ref[...].astype(jnp.float32) + (first * a + second * b)).astype(
        jnp.bfloat16
    )


def whole_spec(*shape):
    return pl.BlockSpec(shape, lambda i: (0,) * len(shape))


def run_scan(x, dt, w_dt, bias, a_log, b_wide, c_wide, span):
    tokens, channels = x.shape
    rank, nstate = dt.shape[1], a_log.shape[0]
    cols = lambda rows: pl.BlockSpec((rows, span), lambda i: (0, i))
    return pl.pallas_call(
        scan_kernel,
        grid=(channels // span,),
        in_specs=[
            cols(tokens),
            whole_spec(tokens, rank),
            cols(rank),
            cols(1),
            cols(nstate),
            whole_spec(tokens, nstate, LANES),
            whole_spec(tokens, nstate, LANES),
        ],
        out_specs=[cols(tokens), cols(tokens), cols(nstate)],
        out_shape=[
            jax.ShapeDtypeStruct((tokens, channels), jnp.float32),
            jax.ShapeDtypeStruct((tokens, channels), jnp.float32),
            jax.ShapeDtypeStruct((nstate, channels), jnp.float32),
        ],
        scratch_shapes=[
            pltpu.VMEM((tokens, span), jnp.float32),
            pltpu.VMEM((tokens, span), jnp.float32),
        ],
        compiler_params=pltpu.CompilerParams(vmem_limit_bytes=32 * 1024 * 1024),
        name="scan_local",
    )(x, dt, w_dt, bias[None], a_log, b_wide, c_wide)


def run_mix(x, y, cum, a_log, start, c_wide, skip, pack, span):
    tokens, channels = x.shape
    nstate, slots = a_log.shape[0], pack.shape[0]
    cols = lambda rows: pl.BlockSpec((rows, span), lambda i: (0, i))
    return pl.pallas_call(
        mix_kernel,
        grid=(channels // span,),
        in_specs=[
            cols(tokens),
            cols(tokens),
            cols(tokens),
            cols(nstate),
            cols(nstate),
            whole_spec(tokens, nstate, LANES),
            cols(1),
            whole_spec(slots, tokens),
        ],
        out_specs=[cols(tokens), cols(slots)],
        out_shape=[
            jax.ShapeDtypeStruct((tokens, channels), jnp.bfloat16),
            jax.ShapeDtypeStruct((slots, channels), jnp.bfloat16),
        ],
        scratch_shapes=[pltpu.VMEM((tokens, span), jnp.float32)],
        compiler_params=pltpu.CompilerParams(vmem_limit_bytes=32 * 1024 * 1024),
        name="mix_pack",
    )(x, y, cum, a_log, start, c_wide, skip[None], pack)


def run_final(mixer, back, one, two, weights, span):
    tokens, channels = mixer.shape
    slots = back.shape[0]
    cols = lambda rows: pl.BlockSpec((rows, span), lambda i: (0, i))
    return pl.pallas_call(
        final_kernel,
        grid=(channels // span,),
        in_specs=[
            cols(tokens),
            cols(slots),
            whole_spec(tokens, slots),
            whole_spec(tokens, slots),
            whole_spec(tokens, 2),
        ],
        out_specs=cols(tokens),
        out_shape=jax.ShapeDtypeStruct((tokens, channels), jnp.bfloat16),
        compiler_params=pltpu.CompilerParams(vmem_limit_bytes=32 * 1024 * 1024),
        name="final_sum",
    )(mixer, back, one, two, weights)


def shift(value, by):
    count = lax.axis_size("seq")
    return lax.ppermute(value, "seq", [(i, i + by) for i in range(count - by)])


def carry_in(a_neg, total, end_state):
    count = lax.axis_size("seq")
    both = jnp.concatenate([end_state, total], axis=0)
    start = jnp.zeros_like(end_state)
    between = jnp.zeros_like(total)
    if count <= 4:
        arrived = [shift(both, by) for by in range(1, count)]
        for item in arrived:
            start = start + jnp.exp(a_neg * between) * item[:-1]
            between = between + item[-1:]
        return start

    def relay(index, incoming):
        return shift(jnp.exp(a_neg * total) * incoming + end_state, 1)

    return lax.fori_loop(0, count - 1, relay, start)


def routing(picks, groups, rows):
    tokens = picks.shape[0]
    flat = picks.reshape(-1)
    onehot = (flat[:, None] == jnp.arange(groups, dtype=jnp.int32)[None, :]).astype(jnp.float32)
    steps = jnp.arange(2 * tokens, dtype=jnp.int32)
    earlier = (steps[:, None] > steps[None, :]).astype(jnp.float32)
    before = jnp.dot(earlier, onehot, preferred_element_type=jnp.float32)
    position = jnp.sum(onehot * before, axis=1).astype(jnp.int32)
    place = (flat * rows + position).reshape(tokens, 2)
    slots = jnp.arange(groups * rows, dtype=jnp.int32)
    one = (place[:, 0:1] == slots[None, :]).astype(jnp.bfloat16)
    two = (place[:, 1:2] == slots[None, :]).astype(jnp.bfloat16)
    pack = (
        (place[:, 0][None, :] == slots[:, None]) | (place[:, 1][None, :] == slots[:, None])
    ).astype(jnp.bfloat16)
    return one, two, pack


def per_device(
    x_act, dt_low, b_c, w_dt, dt_bias, a_log, d_skip, w_router, expert_ids, w_up, w_down
):
    x, dt = x_act[0], dt_low[0]
    tokens, channels = x.shape
    nstate = a_log.shape[0]
    groups = w_router.shape[0]
    owners = lax.axis_size("exp")
    capacity = 5 * tokens // owners
    rows = -(-capacity // 16) * 16
    span = 512
    picks = expert_ids[0]
    up = lax.all_gather(w_up, "seq", axis=1, tiled=True)[0]
    down = lax.all_gather(w_down, "seq", axis=2, tiled=True)[0]
    one, two, pack = routing(picks, groups, rows)
    wide = jnp.broadcast_to(b_c[0][:, :, None], b_c.shape[1:] + (LANES,))
    b_wide, c_wide = wide[:, :nstate], wide[:, nstate:]
    y, cum, end_state = run_scan(x, dt, w_dt, dt_bias, a_log, b_wide, c_wide, span)
    start = carry_in(-jnp.exp(a_log), cum[-1:], end_state)
    mixer, packed = run_mix(x, y, cum, a_log, start, c_wide, d_skip, pack, span)

    logits = jnp.dot(mixer, w_router.T, preferred_element_type=jnp.float32)
    ids = jnp.arange(groups, dtype=jnp.int32)
    gap = jnp.sum(
        jnp.where(picks[:, 0:1] == ids, logits, 0.0) - jnp.where(picks[:, 1:2] == ids, logits, 0.0),
        axis=1,
        keepdims=True,
    )
    first = jax.nn.sigmoid(gap)
    weights = jnp.concatenate([first, 1.0 - first], axis=1)

    lanes = [[2 * g + h for g in range(groups)] for h in range(2)]
    swap = [(i, i ^ 1) for i in range(owners)]
    exchange = functools.partial(
        lax.all_to_all, axis_name="exp", split_axis=0, concat_axis=0, axis_index_groups=lanes, tiled=True
    )

    def half(block):
        hidden = jnp.dot(block, up, preferred_element_type=jnp.float32)
        hidden = jax.nn.silu(hidden).astype(jnp.bfloat16)
        return jnp.dot(hidden, down, preferred_element_type=jnp.float32).astype(jnp.bfloat16)

    mine = exchange(packed.reshape(groups, rows, channels)).reshape(-1, channels)
    other = lax.ppermute(mine, "exp", swap)
    theirs = lax.ppermute(half(other), "exp", swap)
    combined = (half(mine).astype(jnp.float32) + theirs.astype(jnp.float32)).astype(jnp.bfloat16)
    back = exchange(combined.reshape(groups, rows, channels)).reshape(-1, channels)
    return run_final(mixer, back, one, two, weights, span)[None]


def solution(mesh):
    in_specs = (
        P("exp", "seq", None),
        P("exp", "seq", None),
        P("exp", "seq", None),
        P(),
        P(),
        P(),
        P(),
        P(),
        P("exp", "seq", None),
        P("exp", "seq", None),
        P("exp", None, "seq"),
    )
    out_specs = P("exp", "seq", None)
    return jax.shard_map(
        per_device, mesh=mesh, in_specs=in_specs, out_specs=out_specs, check_vma=False
    )
```

```python
import functools
import math

import jax
import jax.numpy as jnp
from jax import lax
from jax.experimental import pallas as pl
from jax.experimental.pallas import tpu as pltpu
from jax.sharding import PartitionSpec as P

LANES = 128
LOG2E = 1.0 / math.log(2.0)


def fold(rows):
    sub = lax.broadcasted_iota(jnp.int32, rows[0].shape, 0)
    for bit in (1, 2, 4):
        low = (sub & bit) == 0
        rows = [
            jnp.where(low, a, b) + pltpu.roll(jnp.where(low, b, a), 8 - bit, 0)
            for a, b in zip(rows[0::2], rows[1::2])
        ]
    return rows[0]


def fold_states(value):
    parts = [value[k : k + 8] for k in range(0, value.shape[0], 8)]
    return functools.reduce(jnp.add, parts)


def scan_kernel(
    x_ref, dt_ref, wdt_ref, bias_ref, alog_ref, b_ref, c_ref, y_ref, cum_ref, end_ref, delta_s, driven_s
):
    tokens, channels = x_ref.shape
    tiles = channels // LANES
    v = jnp.dot(dt_ref[...], wdt_ref[...], preferred_element_type=jnp.float32) + bias_ref[...]
    delta = jnp.maximum(v, 0.0) + jnp.log1p(jnp.exp(-jnp.abs(v)))
    delta_s[...] = delta
    driven_s[...] = delta * x_ref[...].astype(jnp.float32)
    rates = [
        -jnp.exp(alog_ref[:, j * LANES : (j + 1) * LANES]) * LOG2E for j in range(tiles)
    ]

    def body(group, carry):
        states, sums = list(carry[0]), list(carry[1])
        base = pl.multiple_of(group * 8, 8)
        partial = [[] for _ in range(tiles)]
        cums = [[] for _ in range(tiles)]
        delta8 = delta_s[pl.ds(base, 8), :]
        driven8 = driven_s[pl.ds(base, 8), :]
        for i in range(8):
            bt = b_ref[base + i]
            ct = c_ref[base + i]
            for j in range(tiles):
                cols = slice(j * LANES, (j + 1) * LANES)
                d = delta8[i : i + 1, cols]
                u = driven8[i : i + 1, cols]
                states[j] = jnp.exp2(rates[j] * d) * states[j] + u * bt
                partial[j].append(fold_states(ct * states[j]))
                sums[j] = sums[j] + d
                cums[j].append(sums[j])
        for j in range(tiles):
            cols = slice(j * LANES, (j + 1) * LANES)
            y_ref[pl.ds(base, 8), cols] = fold(partial[j])
            cum_ref[pl.ds(base, 8), cols] = jnp.concatenate(cums[j], axis=0)
        return tuple(states), tuple(sums)

    nstate = alog_ref.shape[0]
    init = (
        tuple(jnp.zeros((nstate, LANES), jnp.float32) for _ in range(tiles)),
        tuple(jnp.zeros((1, LANES), jnp.float32) for _ in range(tiles)),
    )
    states, _ = lax.fori_loop(0, tokens // 8, body, init)
    for j in range(tiles):
        end_ref[:, j * LANES : (j + 1) * LANES] = states[j]


def mix_kernel(
    x_ref, y_ref, cum_ref, alog_ref, start_ref, c_ref, skip_ref, pack_ref, mixer_ref, packed_ref, y_s
):
    tokens, channels = x_ref.shape
    tiles = channels // LANES
    rates = [
        -jnp.exp(alog_ref[:, j * LANES : (j + 1) * LANES]) * LOG2E for j in range(tiles)
    ]
    starts = [start_ref[:, j * LANES : (j + 1) * LANES] for j in range(tiles)]

    def body(group, carry):
        base = pl.multiple_of(group * 8, 8)
        partial = [[] for _ in range(tiles)]
        cum8 = cum_ref[pl.ds(base, 8), :]
        for i in range(8):
            ct = c_ref[base + i]
            for j in range(tiles):
                cols = slice(j * LANES, (j + 1) * LANES)
                d = cum8[i : i + 1, cols]
                partial[j].append(fold_states(ct * (jnp.exp2(rates[j] * d) * starts[j])))
        for j in range(tiles):
            y_s[pl.ds(base, 8), j * LANES : (j + 1) * LANES] = fold(partial[j])
        return carry

    lax.fori_loop(0, tokens // 8, body, 0)
    mixer = (y_s[...] + y_ref[...] + skip_ref[...] * x_ref[...].astype(jnp.float32)).astype(
        jnp.bfloat16
    )
    mixer_ref[...] = mixer
    packed_ref[...] = jnp.dot(pack_ref[...], mixer, preferred_element_type=jnp.float32).astype(
        jnp.bfloat16
    )


def final_kernel(mixer_ref, back_ref, one_ref, two_ref, w_ref, out_ref):
    back = back_ref[...]
    a = jnp.dot(one_ref[...], back, preferred_element_type=jnp.float32)
    b = jnp.dot(two_ref[...], back, preferred_element_type=jnp.float32)
    first = w_ref[:, 0:1]
    second = w_ref[:, 1:2]
    out_ref[...] = (mixer_ref[...].astype(jnp.float32) + (first * a + second * b)).astype(
        jnp.bfloat16
    )


def expert_kernel(
    packed_ref, up_ref, down_ref, back_ref,
    recv, wu, wd, part, theirs, comb,
    local_sem, z_send, z_recv, f_send, f_recv, p_send, p_recv, r_send, r_recv,
    wy_send, wy_recv, wc_send, wc_recv,
):
    groups, rows, channels = packed_ref.shape
    shards, depth, hidden_units = wu.shape
    lines = shards // 2
    me, here = lax.axis_index("exp"), lax.axis_index("seq")
    z, h = me // 2, lax.rem(me, 2)
    y, core = here // 2, lax.rem(here, 2)
    partner = {"exp": 2 * z + 1 - h}
    sibling = {"seq": 2 * y + 1 - core}
    mesh_id = pl.DeviceIdType.MESH
    weights = ((up_ref, wu), (down_ref, wd))

    def behind(k):
        return lax.rem(z - k + groups, groups)

    def line_behind(j):
        return lax.rem(y - j + lines, lines)

    def remote(src, dst, send, recv_sem, device):
        return pltpu.make_async_remote_copy(
            src_ref=src, dst_ref=dst, send_sem=send, recv_sem=recv_sem,
            device_id=device, device_id_type=mesh_id,
        )

    barrier = pltpu.get_barrier_semaphore()
    for k in range(1, groups):
        pl.semaphore_signal(
            barrier, inc=1, device_id={"exp": 2 * lax.rem(z + k, groups) + h}, device_id_type=mesh_id
        )
    for j in range(1, lines):
        pl.semaphore_signal(
            barrier, inc=1, device_id={"seq": 2 * lax.rem(y + j, lines) + core}, device_id_type=mesh_id
        )
    pl.semaphore_signal(barrier, inc=1, device_id=partner, device_id_type=mesh_id)
    pl.semaphore_signal(barrier, inc=1, device_id=sibling, device_id_type=mesh_id)
    pl.semaphore_wait(barrier, groups + lines)

    own_rows = pltpu.make_async_copy(packed_ref.at[z], recv.at[z, h], local_sem.at[0])
    own_rows.start()

    def z_copy(k):
        to = lax.rem(z + k, groups)
        return remote(
            packed_ref.at[to], recv.at[z, h], z_send.at[k], z_recv.at[z], {"exp": 2 * to + h}
        )

    def wy_copy(w, j):
        src, dst = weights[w]
        to = lax.rem(y + j, lines)
        return remote(
            src, dst.at[here], wy_send.at[w, j], wy_recv.at[w, y], {"seq": 2 * to + core}
        )

    def wc_copy(w, j):
        src, dst = weights[w]
        line = line_behind(j)
        shard = 2 * line + core
        return remote(
            src if j == 0 else dst.at[shard], dst.at[shard],
            wc_send.at[w, j], wc_recv.at[w, line], sibling,
        )

    def f_copy(k):
        src = behind(k)
        return remote(recv.at[src, h], recv.at[src, h], f_send.at[k], f_recv.at[src], partner)

    def p_copy(k):
        src = behind(k)
        return remote(part.at[src, 1 - h], theirs.at[src], p_send.at[k], p_recv.at[src], partner)

    def r_copy(k):
        src = behind(k)
        return remote(
            comb.at[src], back_ref.at[z], r_send.at[k], r_recv.at[z], {"exp": 2 * src + h}
        )

    def wait_into(dst, sem):
        remote(dst, dst, sem, sem, partner).wait_recv()

    for k in range(1, groups):
        z_copy(k).start()
    own_weights = []
    for w, (src, dst) in enumerate(weights):
        own = pltpu.make_async_copy(src, dst.at[here], local_sem.at[1 + w])
        own.start()
        own_weights.append(own)
        for j in range(1, lines):
            wy_copy(w, j).start()
        wc_copy(w, 0).start()

    def forward(k):
        src = behind(k)
        if k == 0:
            own_rows.wait()
        else:
            wait_into(recv.at[src, h], z_recv.at[src])
        f_copy(k).start()

    def relay_weights(w):
        dst = weights[w][1]
        for j in range(1, lines):
            line = line_behind(j)
            wait_into(dst.at[2 * line + core], wy_recv.at[w, line])
            wc_copy(w, j).start()

    def collect_weights(w):
        dst = weights[w][1]
        own_weights[w].wait()
        for j in range(lines):
            line = line_behind(j)
            wait_into(dst.at[2 * line + 1 - core], wc_recv.at[w, line])

    def compute(k):
        src = behind(k)
        wait_into(recv.at[src, 1 - h], f_recv.at[src])

        def up_step(i, acc):
            cols = pl.ds(pl.multiple_of(i * depth, depth), depth)
            block = recv[src, :, :, cols].reshape(2 * rows, depth)
            return acc + jnp.dot(block, wu[i], preferred_element_type=jnp.float32)

        pre = lax.fori_loop(
            0, shards, up_step, jnp.zeros((2 * rows, hidden_units), jnp.float32)
        )
        hidden = (pre / (1.0 + jnp.exp(-pre))).astype(jnp.bfloat16)

        def down_step(i, carry):
            cols = pl.ds(pl.multiple_of(i * depth, depth), depth)
            out = jnp.dot(hidden, wd[i], preferred_element_type=jnp.float32)
            part[src, :, :, cols] = out.astype(jnp.bfloat16).reshape(2, rows, depth)
            return carry

        lax.fori_loop(0, shards, down_step, 0)
        p_copy(k).start()

    def combine(k):
        src = behind(k)
        wait_into(theirs.at[src], p_recv.at[src])

        def add(i, carry):
            cols = pl.ds(pl.multiple_of(i * depth, depth), depth)
            comb[src, :, cols] = (
                part[src, h, :, cols].astype(jnp.float32) + theirs[src, :, cols].astype(jnp.float32)
            ).astype(jnp.bfloat16)
            return carry

        lax.fori_loop(0, shards, add, 0)
        if k == 0:
            pltpu.make_async_copy(comb.at[z], back_ref.at[z], local_sem.at[3]).start()
        else:
            r_copy(k).start()

    for k in range(groups - 2):
        forward(k)
    relay_weights(0)
    forward(groups - 2)
    relay_weights(1)
    collect_weights(0)
    collect_weights(1)
    for k in range(groups):
        if k == 1:
            forward(groups - 1)
        compute(k)
        if k > 0:
            combine(k - 1)
    combine(groups - 1)

    pltpu.make_async_copy(comb.at[z], back_ref.at[z], local_sem.at[3]).wait()
    for k in range(1, groups):
        src = behind(k)
        wait_into(back_ref.at[src], r_recv.at[src])
        z_copy(k).wait_send()
        r_copy(k).wait_send()
    for k in range(groups):
        f_copy(k).wait_send()
        p_copy(k).wait_send()
    for w in range(2):
        for j in range(lines):
            if j > 0:
                wy_copy(w, j).wait_send()
            wc_copy(w, j).wait_send()


def run_experts(packed, w_up, w_down):
    groups, rows, channels = packed.shape
    depth, hidden_units = w_up.shape
    shards = channels // depth
    lines = shards // 2
    dma = pltpu.SemaphoreType.DMA
    any_spec = pl.BlockSpec(memory_space=pl.ANY)
    bf16 = jnp.bfloat16
    return pl.pallas_call(
        expert_kernel,
        in_specs=[any_spec] * 3,
        out_specs=any_spec,
        out_shape=jax.ShapeDtypeStruct(packed.shape, bf16),
        scratch_shapes=[
            pltpu.VMEM((groups, 2, rows, channels), bf16),
            pltpu.VMEM((shards, depth, hidden_units), bf16),
            pltpu.VMEM((shards, hidden_units, depth), bf16),
            pltpu.VMEM((groups, 2, rows, channels), bf16),
            pltpu.VMEM((groups, rows, channels), bf16),
            pltpu.VMEM((groups, rows, channels), bf16),
            dma((4,)),
        ]
        + [dma((groups,)) for _ in range(8)]
        + [dma((2, lines)) for _ in range(4)],
        compiler_params=pltpu.CompilerParams(
            collective_id=0, has_side_effects=True, vmem_limit_bytes=56 * 1024 * 1024
        ),
        name="experts",
    )(packed, w_up, w_down)


def whole_spec(*shape):
    return pl.BlockSpec(shape, lambda i: (0,) * len(shape))


def run_scan(x, dt, w_dt, bias, a_log, b_wide, c_wide, span):
    tokens, channels = x.shape
    rank, nstate = dt.shape[1], a_log.shape[0]
    cols = lambda rows: pl.BlockSpec((rows, span), lambda i: (0, i))
    return pl.pallas_call(
        scan_kernel,
        grid=(channels // span,),
        in_specs=[
            cols(tokens),
            whole_spec(tokens, rank),
            cols(rank),
            cols(1),
            cols(nstate),
            whole_spec(tokens, nstate, LANES),
            whole_spec(tokens, nstate, LANES),
        ],
        out_specs=[cols(tokens), cols(tokens), cols(nstate)],
        out_shape=[
            jax.ShapeDtypeStruct((tokens, channels), jnp.float32),
            jax.ShapeDtypeStruct((tokens, channels), jnp.float32),
            jax.ShapeDtypeStruct((nstate, channels), jnp.float32),
        ],
        scratch_shapes=[
            pltpu.VMEM((tokens, span), jnp.float32),
            pltpu.VMEM((tokens, span), jnp.float32),
        ],
        compiler_params=pltpu.CompilerParams(vmem_limit_bytes=32 * 1024 * 1024),
        name="scan_local",
    )(x, dt, w_dt, bias[None], a_log, b_wide, c_wide)


def run_mix(x, y, cum, a_log, start, c_wide, skip, pack, span):
    tokens, channels = x.shape
    nstate, slots = a_log.shape[0], pack.shape[0]
    cols = lambda rows: pl.BlockSpec((rows, span), lambda i: (0, i))
    return pl.pallas_call(
        mix_kernel,
        grid=(channels // span,),
        in_specs=[
            cols(tokens),
            cols(tokens),
            cols(tokens),
            cols(nstate),
            cols(nstate),
            whole_spec(tokens, nstate, LANES),
            cols(1),
            whole_spec(slots, tokens),
        ],
        out_specs=[cols(tokens), cols(slots)],
        out_shape=[
            jax.ShapeDtypeStruct((tokens, channels), jnp.bfloat16),
            jax.ShapeDtypeStruct((slots, channels), jnp.bfloat16),
        ],
        scratch_shapes=[pltpu.VMEM((tokens, span), jnp.float32)],
        compiler_params=pltpu.CompilerParams(vmem_limit_bytes=32 * 1024 * 1024),
        name="mix_pack",
    )(x, y, cum, a_log, start, c_wide, skip[None], pack)


def run_final(mixer, back, one, two, weights, span):
    tokens, channels = mixer.shape
    slots = back.shape[0]
    cols = lambda rows: pl.BlockSpec((rows, span), lambda i: (0, i))
    return pl.pallas_call(
        final_kernel,
        grid=(channels // span,),
        in_specs=[
            cols(tokens),
            cols(slots),
            whole_spec(tokens, slots),
            whole_spec(tokens, slots),
            whole_spec(tokens, 2),
        ],
        out_specs=cols(tokens),
        out_shape=jax.ShapeDtypeStruct((tokens, channels), jnp.bfloat16),
        compiler_params=pltpu.CompilerParams(vmem_limit_bytes=32 * 1024 * 1024),
        name="final_sum",
    )(mixer, back, one, two, weights)


def shift(value, by):
    count = lax.axis_size("seq")
    return lax.ppermute(value, "seq", [(i, i + by) for i in range(count - by)])


def carry_in(a_neg, total, end_state):
    count = lax.axis_size("seq")
    both = jnp.concatenate([end_state, total], axis=0)
    start = jnp.zeros_like(end_state)
    between = jnp.zeros_like(total)
    if count <= 4:
        arrived = [shift(both, by) for by in range(1, count)]
        for item in arrived:
            start = start + jnp.exp(a_neg * between) * item[:-1]
            between = between + item[-1:]
        return start

    def relay(index, incoming):
        return shift(jnp.exp(a_neg * total) * incoming + end_state, 1)

    return lax.fori_loop(0, count - 1, relay, start)


def routing(picks, groups, rows):
    tokens = picks.shape[0]
    flat = picks.reshape(-1)
    onehot = (flat[:, None] == jnp.arange(groups, dtype=jnp.int32)[None, :]).astype(jnp.float32)
    steps = jnp.arange(2 * tokens, dtype=jnp.int32)
    earlier = (steps[:, None] > steps[None, :]).astype(jnp.float32)
    before = jnp.dot(earlier, onehot, preferred_element_type=jnp.float32)
    position = jnp.sum(onehot * before, axis=1).astype(jnp.int32)
    place = (flat * rows + position).reshape(tokens, 2)
    slots = jnp.arange(groups * rows, dtype=jnp.int32)
    one = (place[:, 0:1] == slots[None, :]).astype(jnp.bfloat16)
    two = (place[:, 1:2] == slots[None, :]).astype(jnp.bfloat16)
    pack = (
        (place[:, 0][None, :] == slots[:, None]) | (place[:, 1][None, :] == slots[:, None])
    ).astype(jnp.bfloat16)
    return one, two, pack


def per_device(
    x_act, dt_low, b_c, w_dt, dt_bias, a_log, d_skip, w_router, expert_ids, w_up, w_down
):
    x, dt = x_act[0], dt_low[0]
    tokens, channels = x.shape
    nstate = a_log.shape[0]
    groups = w_router.shape[0]
    owners = lax.axis_size("exp")
    capacity = 5 * tokens // owners
    rows = -(-capacity // 16) * 16
    span = 512
    picks = expert_ids[0]
    one, two, pack = routing(picks, groups, rows)
    wide = jnp.broadcast_to(b_c[0][:, :, None], b_c.shape[1:] + (LANES,))
    b_wide, c_wide = wide[:, :nstate], wide[:, nstate:]
    y, cum, end_state = run_scan(x, dt, w_dt, dt_bias, a_log, b_wide, c_wide, span)
    start = carry_in(-jnp.exp(a_log), cum[-1:], end_state)
    mixer, packed = run_mix(x, y, cum, a_log, start, c_wide, d_skip, pack, span)

    logits = jnp.dot(mixer, w_router.T, preferred_element_type=jnp.float32)
    ids = jnp.arange(groups, dtype=jnp.int32)
    gap = jnp.sum(
        jnp.where(picks[:, 0:1] == ids, logits, 0.0) - jnp.where(picks[:, 1:2] == ids, logits, 0.0),
        axis=1,
        keepdims=True,
    )
    first = jax.nn.sigmoid(gap)
    weights = jnp.concatenate([first, 1.0 - first], axis=1)

    back = run_experts(packed.reshape(groups, rows, channels), w_up[0], w_down[0])
    back = back.reshape(-1, channels)
    return run_final(mixer, back, one, two, weights, span)[None]


def solution(mesh):
    in_specs = (
        P("exp", "seq", None),
        P("exp", "seq", None),
        P("exp", "seq", None),
        P(),
        P(),
        P(),
        P(),
        P(),
        P("exp", "seq", None),
        P("exp", "seq", None),
        P("exp", None, "seq"),
    )
    out_specs = P("exp", "seq", None)
    return jax.shard_map(
        per_device, mesh=mesh, in_specs=in_specs, out_specs=out_specs, check_vma=False
    )
```

```python
import functools
import math

import jax
import jax.numpy as jnp
from jax import lax
from jax.experimental import pallas as pl
from jax.experimental.pallas import tpu as pltpu
from jax.sharding import PartitionSpec as P

LANES = 128
LOG2E = 1.0 / math.log(2.0)


def fold(rows):
    sub = lax.broadcasted_iota(jnp.int32, rows[0].shape, 0)
    for bit in (1, 2, 4):
        low = (sub & bit) == 0
        rows = [
            jnp.where(low, a, b) + pltpu.roll(jnp.where(low, b, a), 8 - bit, 0)
            for a, b in zip(rows[0::2], rows[1::2])
        ]
    return rows[0]


def fold_states(value):
    parts = [value[k : k + 8] for k in range(0, value.shape[0], 8)]
    return functools.reduce(jnp.add, parts)


def scan_kernel(
    x_ref, dt_ref, wdt_ref, bias_ref, alog_ref, b_ref, c_ref, y_ref, cum_ref, end_ref, delta_s, driven_s
):
    tokens, channels = x_ref.shape
    tiles = channels // LANES
    v = jnp.dot(dt_ref[...], wdt_ref[...], preferred_element_type=jnp.float32) + bias_ref[...]
    delta = jnp.maximum(v, 0.0) + jnp.log1p(jnp.exp(-jnp.abs(v)))
    delta_s[...] = delta
    driven_s[...] = delta * x_ref[...].astype(jnp.float32)
    rates = [
        -jnp.exp(alog_ref[:, j * LANES : (j + 1) * LANES]) * LOG2E for j in range(tiles)
    ]

    def body(group, carry):
        states, sums = list(carry[0]), list(carry[1])
        base = pl.multiple_of(group * 8, 8)
        partial = [[] for _ in range(tiles)]
        cums = [[] for _ in range(tiles)]
        delta8 = delta_s[pl.ds(base, 8), :]
        driven8 = driven_s[pl.ds(base, 8), :]
        for i in range(8):
            bt = b_ref[base + i]
            ct = c_ref[base + i]
            for j in range(tiles):
                cols = slice(j * LANES, (j + 1) * LANES)
                d = delta8[i : i + 1, cols]
                u = driven8[i : i + 1, cols]
                states[j] = jnp.exp2(rates[j] * d) * states[j] + u * bt
                partial[j].append(fold_states(ct * states[j]))
                sums[j] = sums[j] + d
                cums[j].append(sums[j])
        for j in range(tiles):
            cols = slice(j * LANES, (j + 1) * LANES)
            y_ref[pl.ds(base, 8), cols] = fold(partial[j])
            cum_ref[pl.ds(base, 8), cols] = jnp.concatenate(cums[j], axis=0)
        return tuple(states), tuple(sums)

    nstate = alog_ref.shape[0]
    init = (
        tuple(jnp.zeros((nstate, LANES), jnp.float32) for _ in range(tiles)),
        tuple(jnp.zeros((1, LANES), jnp.float32) for _ in range(tiles)),
    )
    states, _ = lax.fori_loop(0, tokens // 8, body, init)
    for j in range(tiles):
        end_ref[:, j * LANES : (j + 1) * LANES] = states[j]


def mix_kernel(
    x_ref, y_ref, cum_ref, alog_ref, start_ref, c_ref, skip_ref, pack_ref, mixer_ref, packed_ref, y_s
):
    tokens, channels = x_ref.shape
    tiles = channels // LANES
    rates = [
        -jnp.exp(alog_ref[:, j * LANES : (j + 1) * LANES]) * LOG2E for j in range(tiles)
    ]
    starts = [start_ref[:, j * LANES : (j + 1) * LANES] for j in range(tiles)]

    def body(group, carry):
        base = pl.multiple_of(group * 8, 8)
        partial = [[] for _ in range(tiles)]
        cum8 = cum_ref[pl.ds(base, 8), :]
        for i in range(8):
            ct = c_ref[base + i]
            for j in range(tiles):
                cols = slice(j * LANES, (j + 1) * LANES)
                d = cum8[i : i + 1, cols]
                partial[j].append(fold_states(ct * (jnp.exp2(rates[j] * d) * starts[j])))
        for j in range(tiles):
            y_s[pl.ds(base, 8), j * LANES : (j + 1) * LANES] = fold(partial[j])
        return carry

    lax.fori_loop(0, tokens // 8, body, 0)
    mixer = (y_s[...] + y_ref[...] + skip_ref[...] * x_ref[...].astype(jnp.float32)).astype(
        jnp.bfloat16
    )
    mixer_ref[...] = mixer
    packed_ref[...] = jnp.dot(pack_ref[...], mixer, preferred_element_type=jnp.float32).astype(
        jnp.bfloat16
    )


def final_kernel(mixer_ref, back_ref, one_ref, two_ref, w_ref, out_ref):
    back = back_ref[...]
    a = jnp.dot(one_ref[...], back, preferred_element_type=jnp.float32)
    b = jnp.dot(two_ref[...], back, preferred_element_type=jnp.float32)
    first = w_ref[:, 0:1]
    second = w_ref[:, 1:2]
    out_ref[...] = (mixer_ref[...].astype(jnp.float32) + (first * a + second * b)).astype(
        jnp.bfloat16
    )


def expert_kernel(
    packed_ref, up_ref, up_x_ref, up_y_ref, down_ref, back_ref,
    recv, wu, wd, comb,
    local_sem, own_sem, up_y_sem, z_send, z_recv, r_send, r_recv,
    x_send, x_recv, y_send, y_recv, c_send, c_recv,
):
    groups, rows, channels = packed_ref.shape
    _, shards, depth, hidden_units = wu.shape
    lines = shards // 2
    me, here = lax.axis_index("exp"), lax.axis_index("seq")
    z, h = me // 2, lax.rem(me, 2)
    y, core = here // 2, lax.rem(here, 2)
    partner = {"exp": 2 * z + 1 - h}
    sibling = {"seq": 2 * y + 1 - core}
    mesh_id = pl.DeviceIdType.MESH

    def behind(k):
        return lax.rem(z - k + groups, groups)

    def line_behind(j):
        return lax.rem(y - j + lines, lines)

    def line_peer(j):
        return {"seq": 2 * lax.rem(y + j, lines) + core}

    def remote(src, dst, send, recv_sem, device):
        return pltpu.make_async_remote_copy(
            src_ref=src, dst_ref=dst, send_sem=send, recv_sem=recv_sem,
            device_id=device, device_id_type=mesh_id,
        )

    def wait_into(dst, sem):
        remote(dst, dst, sem, sem, partner).wait_recv()

    barrier = pltpu.get_barrier_semaphore()
    for k in range(1, groups):
        pl.semaphore_signal(
            barrier, inc=1, device_id={"exp": 2 * lax.rem(z + k, groups) + h}, device_id_type=mesh_id
        )
    for j in range(1, lines):
        pl.semaphore_signal(barrier, inc=1, device_id=line_peer(j), device_id_type=mesh_id)
    pl.semaphore_signal(barrier, inc=1, device_id=partner, device_id_type=mesh_id)
    pl.semaphore_signal(barrier, inc=1, device_id=sibling, device_id_type=mesh_id)
    pl.semaphore_wait(barrier, groups + lines)

    def z_copy(k):
        to = lax.rem(z + k, groups)
        return remote(
            packed_ref.at[to], recv.at[z], z_send.at[k], z_recv.at[z], {"exp": 2 * to + h}
        )

    def r_copy(k):
        src = behind(k)
        return remote(
            comb.at[src], back_ref.at[z], r_send.at[k], r_recv.at[z], {"exp": 2 * src + h}
        )

    def half_of(q):
        return h if q == 0 else 1 - h

    def y_copy(q, j):
        src = down_ref if q == 0 else wd.at[1 - h, here]
        return remote(
            src, wd.at[half_of(q), here], y_send.at[q, j], y_recv.at[q, y], line_peer(j)
        )

    def x_copy(j):
        if j == 0:
            return remote(down_ref, wd.at[h, here], x_send.at[0], x_recv.at[y], partner)
        line = line_behind(j)
        return remote(
            up_y_ref.at[j - 1], wu.at[h, 2 * line + core], x_send.at[j], x_recv.at[line], partner
        )

    def c_copy(w, q, j):
        line = line_behind(j)
        shard = 2 * line + core
        dst = (wu if w == 0 else wd).at[half_of(q), shard]
        if j == 0:
            src = ((up_ref, up_x_ref), (down_ref, dst))[w][q]
        elif w == 0 and q == 0:
            src = up_y_ref.at[j - 1]
        else:
            src = dst
        at = (2 * w + half_of(q)) * lines + line
        return remote(src, dst, c_send.at[(2 * w + q) * lines + j], c_recv.at[at], sibling)

    for k in range(1, groups):
        z_copy(k).start()
    for j in range(1, lines):
        y_copy(0, j).start()
    for j in range(lines):
        x_copy(j).start()
    local = [
        pltpu.make_async_copy(packed_ref.at[z], recv.at[z], local_sem.at[0]),
        pltpu.make_async_copy(up_ref, wu.at[h, here], own_sem.at[0]),
        pltpu.make_async_copy(up_x_ref, wu.at[1 - h, here], own_sem.at[1]),
        pltpu.make_async_copy(down_ref, wd.at[h, here], own_sem.at[2]),
    ]
    for j in range(1, lines):
        local.append(
            pltpu.make_async_copy(
                up_y_ref.at[j - 1], wu.at[h, 2 * line_behind(j) + core], up_y_sem.at[j]
            )
        )
    for copy in local:
        copy.start()
    c_copy(0, 0, 0).start()
    c_copy(0, 1, 0).start()
    c_copy(1, 0, 0).start()
    for j in range(1, lines):
        c_copy(0, 0, j).start()
    wait_into(wd.at[1 - h, here], x_recv.at[y])
    for j in range(1, lines):
        y_copy(1, j).start()
    c_copy(1, 1, 0).start()
    for j in range(1, lines):
        line = line_behind(j)
        wait_into(wu.at[1 - h, 2 * line + core], x_recv.at[line])
        c_copy(0, 1, j).start()
    for q in range(2):
        for j in range(1, lines):
            line = line_behind(j)
            wait_into(wd.at[half_of(q), 2 * line + core], y_recv.at[q, line])
            c_copy(1, q, j).start()
    for copy in local:
        copy.wait()
    for w in range(2):
        for half in range(2):
            for j in range(lines):
                line = line_behind(j)
                wait_into(
                    (wu if w == 0 else wd).at[half, 2 * line + 1 - core],
                    c_recv.at[(2 * w + half) * lines + line],
                )

    def compute(first, second):
        sources = [behind(first), behind(second)]
        for k, src in zip((first, second), sources):
            if k:
                wait_into(recv.at[src], z_recv.at[src])
        zero = jnp.zeros((2 * rows, hidden_units), jnp.float32)

        def up_step(i, acc):
            cols = pl.ds(pl.multiple_of(i * depth, depth), depth)
            block = jnp.concatenate([recv[src, :, cols] for src in sources], axis=0)
            return tuple(
                acc[n] + jnp.dot(block, wu[n, i], preferred_element_type=jnp.float32)
                for n in range(2)
            )

        pre = lax.fori_loop(0, shards, up_step, (zero, zero))
        hidden = [(p / (1.0 + jnp.exp(-p))).astype(jnp.bfloat16) for p in pre]

        def down_step(i, carry):
            cols = pl.ds(pl.multiple_of(i * depth, depth), depth)
            total = sum(
                jnp.dot(hidden[n], wd[n, i], preferred_element_type=jnp.float32)
                .astype(jnp.bfloat16)
                .astype(jnp.float32)
                for n in range(2)
            ).astype(jnp.bfloat16)
            for n, src in enumerate(sources):
                comb[src, :, cols] = total[n * rows : (n + 1) * rows]
            return carry

        lax.fori_loop(0, shards, down_step, 0)
        for k in (first, second):
            if k:
                r_copy(k).start()

    order = list(range(1, groups)) + [0]
    for k in range(0, groups, 2):
        compute(order[k], order[k + 1])
    keep = pltpu.make_async_copy(comb.at[z], back_ref.at[z], local_sem.at[0])
    keep.start()
    keep.wait()
    for k in range(1, groups):
        src = behind(k)
        wait_into(back_ref.at[src], r_recv.at[src])
        z_copy(k).wait_send()
        r_copy(k).wait_send()
    for j in range(lines):
        x_copy(j).wait_send()
    for j in range(1, lines):
        for q in range(2):
            y_copy(q, j).wait_send()
    for w in range(2):
        for q in range(2):
            for j in range(lines):
                c_copy(w, q, j).wait_send()


def run_experts(packed, w_up, up_x, up_y, w_down):
    groups, rows, channels = packed.shape
    depth, hidden_units = w_up.shape
    shards = channels // depth
    lines = shards // 2
    dma = pltpu.SemaphoreType.DMA
    any_spec = pl.BlockSpec(memory_space=pl.ANY)
    bf16 = jnp.bfloat16
    return pl.pallas_call(
        expert_kernel,
        in_specs=[any_spec] * 5,
        out_specs=any_spec,
        out_shape=jax.ShapeDtypeStruct(packed.shape, bf16),
        scratch_shapes=[
            pltpu.VMEM((groups, rows, channels), bf16),
            pltpu.VMEM((2, shards, depth, hidden_units), bf16),
            pltpu.VMEM((2, shards, hidden_units, depth), bf16),
            pltpu.VMEM((groups, rows, channels), bf16),
            dma((1,)),
            dma((3,)),
            dma((lines,)),
        ]
        + [dma((groups,)) for _ in range(4)]
        + [dma((lines,)), dma((lines,)), dma((2, lines)), dma((2, lines))]
        + [dma((4 * lines,)), dma((4 * lines,))],
        compiler_params=pltpu.CompilerParams(
            collective_id=0, has_side_effects=True, vmem_limit_bytes=56 * 1024 * 1024
        ),
        name="experts",
    )(packed, w_up, up_x, up_y, w_down)


def whole_spec(*shape):
    return pl.BlockSpec(shape, lambda i: (0,) * len(shape))


def vector_cost(updates):
    return pl.CostEstimate(flops=2048 * updates, bytes_accessed=6 * updates, transcendentals=updates)


def run_scan(x, dt, w_dt, bias, a_log, b_wide, c_wide, span):
    tokens, channels = x.shape
    rank, nstate = dt.shape[1], a_log.shape[0]
    cols = lambda rows: pl.BlockSpec((rows, span), lambda i: (0, i))
    return pl.pallas_call(
        scan_kernel,
        grid=(channels // span,),
        in_specs=[
            cols(tokens),
            whole_spec(tokens, rank),
            cols(rank),
            cols(1),
            cols(nstate),
            whole_spec(tokens, nstate, LANES),
            whole_spec(tokens, nstate, LANES),
        ],
        out_specs=[cols(tokens), cols(tokens), cols(nstate)],
        out_shape=[
            jax.ShapeDtypeStruct((tokens, channels), jnp.float32),
            jax.ShapeDtypeStruct((tokens, channels), jnp.float32),
            jax.ShapeDtypeStruct((nstate, channels), jnp.float32),
        ],
        scratch_shapes=[
            pltpu.VMEM((tokens, span), jnp.float32),
            pltpu.VMEM((tokens, span), jnp.float32),
        ],
        compiler_params=pltpu.CompilerParams(vmem_limit_bytes=32 * 1024 * 1024),
        cost_estimate=vector_cost(tokens * nstate * channels),
        name="scan_local",
    )(x, dt, w_dt, bias[None], a_log, b_wide, c_wide)


def run_mix(x, y, cum, a_log, start, c_wide, skip, pack, span):
    tokens, channels = x.shape
    nstate, slots = a_log.shape[0], pack.shape[0]
    cols = lambda rows: pl.BlockSpec((rows, span), lambda i: (0, i))
    return pl.pallas_call(
        mix_kernel,
        grid=(channels // span,),
        in_specs=[
            cols(tokens),
            cols(tokens),
            cols(tokens),
            cols(nstate),
            cols(nstate),
            whole_spec(tokens, nstate, LANES),
            cols(1),
            whole_spec(slots, tokens),
        ],
        out_specs=[cols(tokens), cols(slots)],
        out_shape=[
            jax.ShapeDtypeStruct((tokens, channels), jnp.bfloat16),
            jax.ShapeDtypeStruct((slots, channels), jnp.bfloat16),
        ],
        scratch_shapes=[pltpu.VMEM((tokens, span), jnp.float32)],
        compiler_params=pltpu.CompilerParams(vmem_limit_bytes=32 * 1024 * 1024),
        cost_estimate=vector_cost(tokens * nstate * channels),
        name="mix_pack",
    )(x, y, cum, a_log, start, c_wide, skip[None], pack)


def run_final(mixer, back, one, two, weights, span):
    tokens, channels = mixer.shape
    slots = back.shape[0]
    cols = lambda rows: pl.BlockSpec((rows, span), lambda i: (0, i))
    return pl.pallas_call(
        final_kernel,
        grid=(channels // span,),
        in_specs=[
            cols(tokens),
            cols(slots),
            whole_spec(tokens, slots),
            whole_spec(tokens, slots),
            whole_spec(tokens, 2),
        ],
        out_specs=cols(tokens),
        out_shape=jax.ShapeDtypeStruct((tokens, channels), jnp.bfloat16),
        compiler_params=pltpu.CompilerParams(vmem_limit_bytes=32 * 1024 * 1024),
        name="final_sum",
    )(mixer, back, one, two, weights)


def shift(value, by):
    count = lax.axis_size("seq")
    return lax.ppermute(value, "seq", [(i, i + by) for i in range(count - by)])


def carry_in(a_neg, total, end_state):
    count = lax.axis_size("seq")
    both = jnp.concatenate([end_state, total], axis=0)
    start = jnp.zeros_like(end_state)
    between = jnp.zeros_like(total)
    if count <= 4:
        arrived = [shift(both, by) for by in range(1, count)]
        for item in arrived:
            start = start + jnp.exp(a_neg * between) * item[:-1]
            between = between + item[-1:]
        return start

    def relay(index, incoming):
        return shift(jnp.exp(a_neg * total) * incoming + end_state, 1)

    return lax.fori_loop(0, count - 1, relay, start)


def routing(picks, groups, rows):
    tokens = picks.shape[0]
    flat = picks.reshape(-1)
    onehot = (flat[:, None] == jnp.arange(groups, dtype=jnp.int32)[None, :]).astype(jnp.float32)
    steps = jnp.arange(2 * tokens, dtype=jnp.int32)
    earlier = (steps[:, None] > steps[None, :]).astype(jnp.float32)
    before = jnp.dot(earlier, onehot, preferred_element_type=jnp.float32)
    position = jnp.sum(onehot * before, axis=1).astype(jnp.int32)
    place = (flat * rows + position).reshape(tokens, 2)
    slots = jnp.arange(groups * rows, dtype=jnp.int32)
    one = (place[:, 0:1] == slots[None, :]).astype(jnp.bfloat16)
    two = (place[:, 1:2] == slots[None, :]).astype(jnp.bfloat16)
    pack = (
        (place[:, 0][None, :] == slots[:, None]) | (place[:, 1][None, :] == slots[:, None])
    ).astype(jnp.bfloat16)
    return one, two, pack


def per_device(
    x_act, dt_low, b_c, w_dt, dt_bias, a_log, d_skip, w_router, expert_ids, w_up, w_down
):
    x, dt = x_act[0], dt_low[0]
    tokens, channels = x.shape
    nstate = a_log.shape[0]
    groups = w_router.shape[0]
    owners = lax.axis_size("exp")
    capacity = 5 * tokens // owners
    rows = -(-capacity // 16) * 16
    span = 512
    picks = expert_ids[0]
    swap = [(i, i ^ 1) for i in range(owners)]
    up_x = lax.ppermute(w_up[0], "exp", swap)
    ring = lax.axis_size("seq")
    up_y = jnp.stack(
        [
            lax.ppermute(w_up[0], "seq", [(i, (i + by) % ring) for i in range(ring)])
            for by in range(2, ring, 2)
        ]
    )
    one, two, pack = routing(picks, groups, rows)
    wide = jnp.broadcast_to(b_c[0][:, :, None], b_c.shape[1:] + (LANES,))
    b_wide, c_wide = wide[:, :nstate], wide[:, nstate:]
    y, cum, end_state = run_scan(x, dt, w_dt, dt_bias, a_log, b_wide, c_wide, span)
    start = carry_in(-jnp.exp(a_log), cum[-1:], end_state)
    mixer, packed = run_mix(x, y, cum, a_log, start, c_wide, d_skip, pack, span)

    logits = jnp.dot(mixer, w_router.T, preferred_element_type=jnp.float32)
    ids = jnp.arange(groups, dtype=jnp.int32)
    gap = jnp.sum(
        jnp.where(picks[:, 0:1] == ids, logits, 0.0) - jnp.where(picks[:, 1:2] == ids, logits, 0.0),
        axis=1,
        keepdims=True,
    )
    first = jax.nn.sigmoid(gap)
    weights = jnp.concatenate([first, 1.0 - first], axis=1)

    back = run_experts(
        packed.reshape(groups, rows, channels), w_up[0], up_x, up_y, w_down[0]
    )
    back = back.reshape(-1, channels)
    return run_final(mixer, back, one, two, weights, span)[None]


def solution(mesh):
    in_specs = (
        P("exp", "seq", None),
        P("exp", "seq", None),
        P("exp", "seq", None),
        P(),
        P(),
        P(),
        P(),
        P(),
        P("exp", "seq", None),
        P("exp", "seq", None),
        P("exp", None, "seq"),
    )
    out_specs = P("exp", "seq", None)
    return jax.shard_map(
        per_device, mesh=mesh, in_specs=in_specs, out_specs=out_specs, check_vma=False
    )
```

```python
import functools
import math

import jax
import jax.numpy as jnp
from jax import lax
from jax.experimental import pallas as pl
from jax.experimental.pallas import tpu as pltpu
from jax.sharding import PartitionSpec as P

LANES = 128
LOG2E = 1.0 / math.log(2.0)


def fold(rows):
    sub = lax.broadcasted_iota(jnp.int32, rows[0].shape, 0)
    for bit in (1, 2, 4):
        low = (sub & bit) == 0
        rows = [
            jnp.where(low, a, b) + pltpu.roll(jnp.where(low, b, a), 8 - bit, 0)
            for a, b in zip(rows[0::2], rows[1::2])
        ]
    return rows[0]


def fold_states(value):
    parts = [value[k : k + 8] for k in range(0, value.shape[0], 8)]
    return functools.reduce(jnp.add, parts)


def scan_kernel(
    x_ref, dt_ref, wdt_ref, bias_ref, alog_ref, b_ref, c_ref, y_ref, cum_ref, end_ref, delta_s, driven_s
):
    tokens, channels = x_ref.shape
    tiles = channels // LANES
    v = jnp.dot(dt_ref[...], wdt_ref[...], preferred_element_type=jnp.float32) + bias_ref[...]
    delta = jnp.maximum(v, 0.0) + jnp.log1p(jnp.exp(-jnp.abs(v)))
    delta_s[...] = delta
    driven_s[...] = delta * x_ref[...].astype(jnp.float32)
    rates = [
        -jnp.exp(alog_ref[:, j * LANES : (j + 1) * LANES]) * LOG2E for j in range(tiles)
    ]

    def body(group, carry):
        states, sums = list(carry[0]), list(carry[1])
        base = pl.multiple_of(group * 8, 8)
        partial = [[] for _ in range(tiles)]
        cums = [[] for _ in range(tiles)]
        delta8 = delta_s[pl.ds(base, 8), :]
        driven8 = driven_s[pl.ds(base, 8), :]
        for i in range(8):
            bt = b_ref[base + i]
            ct = c_ref[base + i]
            for j in range(tiles):
                cols = slice(j * LANES, (j + 1) * LANES)
                d = delta8[i : i + 1, cols]
                u = driven8[i : i + 1, cols]
                states[j] = jnp.exp2(rates[j] * d) * states[j] + u * bt
                partial[j].append(fold_states(ct * states[j]))
                sums[j] = sums[j] + d
                cums[j].append(sums[j])
        for j in range(tiles):
            cols = slice(j * LANES, (j + 1) * LANES)
            y_ref[pl.ds(base, 8), cols] = fold(partial[j])
            cum_ref[pl.ds(base, 8), cols] = jnp.concatenate(cums[j], axis=0)
        return tuple(states), tuple(sums)

    nstate = alog_ref.shape[0]
    init = (
        tuple(jnp.zeros((nstate, LANES), jnp.float32) for _ in range(tiles)),
        tuple(jnp.zeros((1, LANES), jnp.float32) for _ in range(tiles)),
    )
    states, _ = lax.fori_loop(0, tokens // 8, body, init)
    for j in range(tiles):
        end_ref[:, j * LANES : (j + 1) * LANES] = states[j]


def mix_columns(
    column, span, x_ref, y_ref, cum_ref, alog_ref, start_ref, c_ref, skip_ref, pack_ref, mixer_ref, packed, y_s
):
    tokens = x_ref.shape[0]
    groups, rows, _ = packed.shape
    tiles = span // LANES
    lanes = [pl.ds(pl.multiple_of(column + j * LANES, LANES), LANES) for j in range(tiles)]
    every = pl.ds(pl.multiple_of(column, span), span)
    rates = [-jnp.exp(alog_ref[:, at]) * LOG2E for at in lanes]
    starts = [start_ref[:, at] for at in lanes]

    def body(group, carry):
        base = pl.multiple_of(group * 8, 8)
        partial = [[] for _ in range(tiles)]
        cum8 = cum_ref[pl.ds(base, 8), every]
        for i in range(8):
            ct = c_ref[base + i]
            for j in range(tiles):
                d = cum8[i : i + 1, j * LANES : (j + 1) * LANES]
                partial[j].append(fold_states(ct * (jnp.exp2(rates[j] * d) * starts[j])))
        for j in range(tiles):
            y_s[pl.ds(base, 8), j * LANES : (j + 1) * LANES] = fold(partial[j])
        return carry

    lax.fori_loop(0, tokens // 8, body, 0)
    mixer = (
        y_s[...] + y_ref[:, every] + skip_ref[:, every] * x_ref[:, every].astype(jnp.float32)
    ).astype(jnp.bfloat16)
    mixer_ref[:, every] = mixer
    packed[:, :, every] = (
        jnp.dot(pack_ref[...], mixer, preferred_element_type=jnp.float32)
        .astype(jnp.bfloat16)
        .reshape(groups, rows, span)
    )


def final_kernel(mixer_ref, back_ref, one_ref, two_ref, w_ref, out_ref):
    back = back_ref[...]
    a = jnp.dot(one_ref[...], back, preferred_element_type=jnp.float32)
    b = jnp.dot(two_ref[...], back, preferred_element_type=jnp.float32)
    first = w_ref[:, 0:1]
    second = w_ref[:, 1:2]
    out_ref[...] = (mixer_ref[...].astype(jnp.float32) + (first * a + second * b)).astype(
        jnp.bfloat16
    )


def expert_kernel(
    x_in, y_in, cum_in, alog_in, start_in, c_in, skip_in, pack_in,
    up_ref, up_x_ref, down_ref, back_ref, mixer_ref,
    packed, recv, wu, wd, comb, y_s,
    local_sem, own_sem, z_send, z_recv, r_send, r_recv,
    x_send, x_recv, y_send, y_recv, c_send, c_recv,
):
    groups, rows, channels = packed.shape
    _, shards, depth, hidden_units = wu.shape
    lines = shards // 2
    me, here = lax.axis_index("exp"), lax.axis_index("seq")
    z, h = me // 2, lax.rem(me, 2)
    y, core = here // 2, lax.rem(here, 2)
    partner = {"exp": 2 * z + 1 - h}
    sibling = {"seq": 2 * y + 1 - core}
    mesh_id = pl.DeviceIdType.MESH

    def behind(k):
        return lax.rem(z - k + groups, groups)

    def line_behind(j):
        return lax.rem(y - j + lines, lines)

    def line_peer(j):
        return {"seq": 2 * lax.rem(y + j, lines) + core}

    def remote(src, dst, send, recv_sem, device):
        return pltpu.make_async_remote_copy(
            src_ref=src, dst_ref=dst, send_sem=send, recv_sem=recv_sem,
            device_id=device, device_id_type=mesh_id,
        )

    def wait_into(dst, sem):
        remote(dst, dst, sem, sem, partner).wait_recv()

    barrier = pltpu.get_barrier_semaphore()
    for k in range(1, groups):
        pl.semaphore_signal(
            barrier, inc=1, device_id={"exp": 2 * lax.rem(z + k, groups) + h}, device_id_type=mesh_id
        )
    for j in range(1, lines):
        pl.semaphore_signal(barrier, inc=1, device_id=line_peer(j), device_id_type=mesh_id)
    pl.semaphore_signal(barrier, inc=1, device_id=partner, device_id_type=mesh_id)
    pl.semaphore_signal(barrier, inc=1, device_id=sibling, device_id_type=mesh_id)
    pl.semaphore_wait(barrier, groups + lines)

    def columns(i):
        return pl.ds(pl.multiple_of(i * depth, depth), depth)

    def z_copy(k, i):
        to = lax.rem(z + k, groups)
        return remote(
            packed.at[to, :, columns(i)],
            recv.at[z, :, columns(i)],
            z_send.at[k * shards + i],
            z_recv.at[z * shards + i],
            {"exp": 2 * to + h},
        )

    def r_copy(k, i):
        src = behind(k)
        return remote(
            comb.at[src, :, columns(i)],
            back_ref.at[z, :, columns(i)],
            r_send.at[k * shards + i],
            r_recv.at[z * shards + i],
            {"exp": 2 * src + h},
        )

    def half_of(q):
        return h if q == 0 else 1 - h

    cut = hidden_units // 32 * 16

    def y_copy(kind, j):
        src, dst = (
            (up_ref, wu.at[h, here]),
            (down_ref, wd.at[h, here]),
            (wd.at[1 - h, here, pl.ds(0, cut)], wd.at[1 - h, here, pl.ds(0, cut)]),
        )[kind]
        return remote(src, dst, y_send.at[kind, j], y_recv.at[kind, y], line_peer(j))

    def x_copy(kind, j):
        line = line_behind(j)
        shard = 2 * line + core
        low = wd.at[h, shard, pl.ds(cut, hidden_units - cut)]
        src, dst = ((down_ref, wd.at[h, here]), (wu.at[h, shard], wu.at[h, shard]), (low, low))[kind]
        return remote(src, dst, x_send.at[kind, j], x_recv.at[kind, line], partner)

    def c_copy(w, q, j):
        line = line_behind(j)
        shard = 2 * line + core
        dst = (wu if w == 0 else wd).at[half_of(q), shard]
        src = ((up_ref, up_x_ref), (down_ref, dst))[w][q] if j == 0 else dst
        at = (2 * w + half_of(q)) * lines + line
        return remote(src, dst, c_send.at[(2 * w + q) * lines + j], c_recv.at[at], sibling)

    for j in range(1, lines):
        y_copy(0, j).start()
    x_copy(0, 0).start()
    local = [
        pltpu.make_async_copy(up_ref, wu.at[h, here], own_sem.at[0]),
        pltpu.make_async_copy(up_x_ref, wu.at[1 - h, here], own_sem.at[1]),
        pltpu.make_async_copy(down_ref, wd.at[h, here], own_sem.at[2]),
    ]
    for copy in local:
        copy.start()
    c_copy(0, 0, 0).start()
    c_copy(0, 1, 0).start()
    c_copy(1, 0, 0).start()

    span = y_s.shape[1]

    def mix_step(i, carry):
        def inner(n, inner_carry):
            mix_columns(
                i * depth + n * span, span, x_in, y_in, cum_in, alog_in, start_in, c_in, skip_in,
                pack_in, mixer_ref, packed, y_s,
            )
            return inner_carry

        lax.fori_loop(0, depth // span, inner, 0)
        for k in range(1, groups):
            z_copy(k, i).start()
        return carry

    lax.fori_loop(0, shards, mix_step, 0)

    for j in range(1, lines):
        line = line_behind(j)
        wait_into(wu.at[h, 2 * line + core], y_recv.at[0, line])
        y_copy(1, j).start()
        x_copy(1, j).start()
        c_copy(0, 0, j).start()
    wait_into(wd.at[1 - h, here], x_recv.at[0, y])
    for j in range(1, lines):
        y_copy(2, j).start()
    c_copy(1, 1, 0).start()
    for j in range(1, lines):
        line = line_behind(j)
        shard = 2 * line + core
        wait_into(wd.at[h, shard], y_recv.at[1, line])
        x_copy(2, j).start()
        c_copy(1, 0, j).start()
    for j in range(1, lines):
        line = line_behind(j)
        shard = 2 * line + core
        wait_into(wu.at[1 - h, shard], x_recv.at[1, line])
        c_copy(0, 1, j).start()
    for j in range(1, lines):
        line = line_behind(j)
        shard = 2 * line + core
        wait_into(wd.at[1 - h, shard, pl.ds(0, cut)], y_recv.at[2, line])
        wait_into(wd.at[1 - h, shard, pl.ds(cut, hidden_units - cut)], x_recv.at[2, line])
        c_copy(1, 1, j).start()
    for copy in local:
        copy.wait()
    for w in range(2):
        for half in range(2):
            for j in range(lines):
                line = line_behind(j)
                wait_into(
                    (wu if w == 0 else wd).at[half, 2 * line + 1 - core],
                    c_recv.at[(2 * w + half) * lines + line],
                )

    def compute(first, second):
        sources = [behind(first), behind(second)]
        zero = jnp.zeros((2 * rows, hidden_units), jnp.float32)

        def up_step(i, acc):
            cols = columns(i)
            for k, src in zip((first, second), sources):
                if k:
                    wait_into(recv.at[src, :, cols], z_recv.at[src * shards + i])
            block = jnp.concatenate(
                [
                    (recv if k else packed)[src, :, cols]
                    for k, src in zip((first, second), sources)
                ],
                axis=0,
            )
            return tuple(
                acc[n] + jnp.dot(block, wu[n, i], preferred_element_type=jnp.float32)
                for n in range(2)
            )

        pre = lax.fori_loop(0, shards, up_step, (zero, zero))
        hidden = [(p / (1.0 + jnp.exp(-p))).astype(jnp.bfloat16) for p in pre]

        def down_step(i, carry):
            cols = columns(i)
            total = sum(
                jnp.dot(hidden[n], wd[n, i], preferred_element_type=jnp.float32)
                .astype(jnp.bfloat16)
                .astype(jnp.float32)
                for n in range(2)
            ).astype(jnp.bfloat16)
            for n, src in enumerate(sources):
                comb[src, :, cols] = total[n * rows : (n + 1) * rows]
            for k in (first, second):
                if k:
                    r_copy(k, i).start()
            return carry

        lax.fori_loop(0, shards, down_step, 0)
    order = list(range(1, groups)) + [0]
    for k in range(0, groups, 2):
        compute(order[k], order[k + 1])
    keep = pltpu.make_async_copy(comb.at[z], back_ref.at[z], local_sem.at[0])
    keep.start()
    keep.wait()
    for k in range(1, groups):
        src = behind(k)

        def finish(i, carry):
            wait_into(back_ref.at[src, :, columns(i)], r_recv.at[src * shards + i])
            z_copy(k, i).wait_send()
            r_copy(k, i).wait_send()
            return carry

        lax.fori_loop(0, shards, finish, 0)
    x_copy(0, 0).wait_send()
    for j in range(1, lines):
        for kind in range(3):
            y_copy(kind, j).wait_send()
        x_copy(1, j).wait_send()
        x_copy(2, j).wait_send()
    for w in range(2):
        for q in range(2):
            for j in range(lines):
                c_copy(w, q, j).wait_send()


def run_experts(mix_inputs, groups, span, w_up, up_x, w_down):
    tokens, channels = mix_inputs[0].shape
    rows = mix_inputs[-1].shape[0] // groups
    depth, hidden_units = w_up.shape
    shards = channels // depth
    lines = shards // 2
    span = min(span, depth)
    dma = pltpu.SemaphoreType.DMA
    any_spec = pl.BlockSpec(memory_space=pl.ANY)
    vmem_spec = pl.BlockSpec(memory_space=pltpu.VMEM)
    bf16 = jnp.bfloat16
    return pl.pallas_call(
        expert_kernel,
        in_specs=[vmem_spec] * len(mix_inputs) + [any_spec] * 3,
        out_specs=[any_spec, vmem_spec],
        out_shape=[
            jax.ShapeDtypeStruct((groups, rows, channels), bf16),
            jax.ShapeDtypeStruct((tokens, channels), bf16),
        ],
        scratch_shapes=[
            pltpu.VMEM((groups, rows, channels), bf16),
            pltpu.VMEM((groups, rows, channels), bf16),
            pltpu.VMEM((2, shards, depth, hidden_units), bf16),
            pltpu.VMEM((2, shards, hidden_units, depth), bf16),
            pltpu.VMEM((groups, rows, channels), bf16),
            pltpu.VMEM((tokens, span), jnp.float32),
            dma((1,)),
            dma((3,)),
        ]
        + [dma((groups * shards,)) for _ in range(4)]
        + [dma((3, lines)) for _ in range(4)]
        + [dma((4 * lines,)), dma((4 * lines,))],
        compiler_params=pltpu.CompilerParams(
            collective_id=0, has_side_effects=True, vmem_limit_bytes=58 * 1024 * 1024
        ),
        name="experts",
    )(*mix_inputs, w_up, up_x, w_down)


def whole_spec(*shape):
    return pl.BlockSpec(shape, lambda i: (0,) * len(shape))


def vector_cost(updates):
    return pl.CostEstimate(flops=2048 * updates, bytes_accessed=6 * updates, transcendentals=updates)


def run_scan(x, dt, w_dt, bias, a_log, b_wide, c_wide, span):
    tokens, channels = x.shape
    rank, nstate = dt.shape[1], a_log.shape[0]
    cols = lambda rows: pl.BlockSpec((rows, span), lambda i: (0, i))
    return pl.pallas_call(
        scan_kernel,
        grid=(channels // span,),
        in_specs=[
            cols(tokens),
            whole_spec(tokens, rank),
            cols(rank),
            cols(1),
            cols(nstate),
            whole_spec(tokens, nstate, LANES),
            whole_spec(tokens, nstate, LANES),
        ],
        out_specs=[cols(tokens), cols(tokens), cols(nstate)],
        out_shape=[
            jax.ShapeDtypeStruct((tokens, channels), jnp.float32),
            jax.ShapeDtypeStruct((tokens, channels), jnp.float32),
            jax.ShapeDtypeStruct((nstate, channels), jnp.float32),
        ],
        scratch_shapes=[
            pltpu.VMEM((tokens, span), jnp.float32),
            pltpu.VMEM((tokens, span), jnp.float32),
        ],
        compiler_params=pltpu.CompilerParams(vmem_limit_bytes=32 * 1024 * 1024),
        cost_estimate=vector_cost(tokens * nstate * channels),
        name="scan_local",
    )(x, dt, w_dt, bias[None], a_log, b_wide, c_wide)


def run_final(mixer, back, one, two, weights, span):
    tokens, channels = mixer.shape
    slots = back.shape[0]
    cols = lambda rows: pl.BlockSpec((rows, span), lambda i: (0, i))
    return pl.pallas_call(
        final_kernel,
        grid=(channels // span,),
        in_specs=[
            cols(tokens),
            cols(slots),
            whole_spec(tokens, slots),
            whole_spec(tokens, slots),
            whole_spec(tokens, 2),
        ],
        out_specs=cols(tokens),
        out_shape=jax.ShapeDtypeStruct((tokens, channels), jnp.bfloat16),
        compiler_params=pltpu.CompilerParams(vmem_limit_bytes=32 * 1024 * 1024),
        name="final_sum",
    )(mixer, back, one, two, weights)


def shift(value, by):
    count = lax.axis_size("seq")
    return lax.ppermute(value, "seq", [(i, i + by) for i in range(count - by)])


def carry_in(a_neg, total, end_state):
    count = lax.axis_size("seq")
    both = jnp.concatenate([end_state, total], axis=0)
    start = jnp.zeros_like(end_state)
    between = jnp.zeros_like(total)
    if count <= 4:
        arrived = [shift(both, by) for by in range(1, count)]
        for item in arrived:
            start = start + jnp.exp(a_neg * between) * item[:-1]
            between = between + item[-1:]
        return start

    def relay(index, incoming):
        return shift(jnp.exp(a_neg * total) * incoming + end_state, 1)

    return lax.fori_loop(0, count - 1, relay, start)


def routing(picks, groups, rows):
    tokens = picks.shape[0]
    flat = picks.reshape(-1)
    onehot = (flat[:, None] == jnp.arange(groups, dtype=jnp.int32)[None, :]).astype(jnp.float32)
    steps = jnp.arange(2 * tokens, dtype=jnp.int32)
    earlier = (steps[:, None] > steps[None, :]).astype(jnp.float32)
    before = jnp.dot(earlier, onehot, preferred_element_type=jnp.float32)
    position = jnp.sum(onehot * before, axis=1).astype(jnp.int32)
    place = (flat * rows + position).reshape(tokens, 2)
    slots = jnp.arange(groups * rows, dtype=jnp.int32)
    one = (place[:, 0:1] == slots[None, :]).astype(jnp.bfloat16)
    two = (place[:, 1:2] == slots[None, :]).astype(jnp.bfloat16)
    pack = (
        (place[:, 0][None, :] == slots[:, None]) | (place[:, 1][None, :] == slots[:, None])
    ).astype(jnp.bfloat16)
    return one, two, pack


def per_device(
    x_act, dt_low, b_c, w_dt, dt_bias, a_log, d_skip, w_router, expert_ids, w_up, w_down
):
    x, dt = x_act[0], dt_low[0]
    tokens, channels = x.shape
    nstate = a_log.shape[0]
    groups = w_router.shape[0]
    owners = lax.axis_size("exp")
    capacity = 5 * tokens // owners
    rows = -(-capacity // 16) * 16
    span = 512
    picks = expert_ids[0]
    swap = [(i, i ^ 1) for i in range(owners)]
    up_x = lax.ppermute(w_up[0], "exp", swap)
    one, two, pack = routing(picks, groups, rows)
    wide = jnp.broadcast_to(b_c[0][:, :, None], b_c.shape[1:] + (LANES,))
    b_wide, c_wide = wide[:, :nstate], wide[:, nstate:]
    y, cum, end_state = run_scan(x, dt, w_dt, dt_bias, a_log, b_wide, c_wide, span)
    start = carry_in(-jnp.exp(a_log), cum[-1:], end_state)
    mix_inputs = (x, y, cum, a_log, start, c_wide, d_skip[None], pack)
    back, mixer = run_experts(mix_inputs, groups, span, w_up[0], up_x, w_down[0])
    logits = jnp.dot(mixer, w_router.T, preferred_element_type=jnp.float32)
    ids = jnp.arange(groups, dtype=jnp.int32)
    gap = jnp.sum(
        jnp.where(picks[:, 0:1] == ids, logits, 0.0) - jnp.where(picks[:, 1:2] == ids, logits, 0.0),
        axis=1,
        keepdims=True,
    )
    first = jax.nn.sigmoid(gap)
    weights = jnp.concatenate([first, 1.0 - first], axis=1)

    back = back.reshape(-1, channels)
    return run_final(mixer, back, one, two, weights, span)[None]


def solution(mesh):
    in_specs = (
        P("exp", "seq", None),
        P("exp", "seq", None),
        P("exp", "seq", None),
        P(),
        P(),
        P(),
        P(),
        P(),
        P("exp", "seq", None),
        P("exp", "seq", None),
        P("exp", None, "seq"),
    )
    out_specs = P("exp", "seq", None)
    return jax.shard_map(
        per_device, mesh=mesh, in_specs=in_specs, out_specs=out_specs, check_vma=False
    )
```

```python
import functools
import math

import jax
import jax.numpy as jnp
from jax import lax
from jax.experimental import pallas as pl
from jax.experimental.pallas import tpu as pltpu
from jax.sharding import PartitionSpec as P

LANES = 128
LOG2E = 1.0 / math.log(2.0)


def fold(rows):
    sub = lax.broadcasted_iota(jnp.int32, rows[0].shape, 0)
    for bit in (1, 2, 4):
        low = (sub & bit) == 0
        rows = [
            jnp.where(low, a, b) + pltpu.roll(jnp.where(low, b, a), 8 - bit, 0)
            for a, b in zip(rows[0::2], rows[1::2])
        ]
    return rows[0]


def fold_states(value):
    parts = [value[k : k + 8] for k in range(0, value.shape[0], 8)]
    return functools.reduce(jnp.add, parts)


def scan_kernel(
    x_ref, dt_ref, wdt_ref, bias_ref, alog_ref, b_ref, c_ref, y_ref, cum_ref, end_ref, delta_s, driven_s
):
    tokens, channels = x_ref.shape
    tiles = channels // LANES
    v = jnp.dot(dt_ref[...], wdt_ref[...], preferred_element_type=jnp.float32) + bias_ref[...]
    delta = jnp.maximum(v, 0.0) + jnp.log1p(jnp.exp(-jnp.abs(v)))
    delta_s[...] = delta
    driven_s[...] = delta * x_ref[...].astype(jnp.float32)
    rates = [
        -jnp.exp(alog_ref[:, j * LANES : (j + 1) * LANES]) * LOG2E for j in range(tiles)
    ]

    def body(group, carry):
        states, sums = list(carry[0]), list(carry[1])
        base = pl.multiple_of(group * 8, 8)
        partial = [[] for _ in range(tiles)]
        cums = [[] for _ in range(tiles)]
        delta8 = delta_s[pl.ds(base, 8), :]
        driven8 = driven_s[pl.ds(base, 8), :]
        for i in range(8):
            bt = b_ref[base + i]
            ct = c_ref[base + i]
            for j in range(tiles):
                cols = slice(j * LANES, (j + 1) * LANES)
                d = delta8[i : i + 1, cols]
                u = driven8[i : i + 1, cols]
                states[j] = jnp.exp2(rates[j] * d) * states[j] + u * bt
                partial[j].append(fold_states(ct * states[j]))
                sums[j] = sums[j] + d
                cums[j].append(sums[j])
        for j in range(tiles):
            cols = slice(j * LANES, (j + 1) * LANES)
            y_ref[pl.ds(base, 8), cols] = fold(partial[j])
            cum_ref[pl.ds(base, 8), cols] = jnp.concatenate(cums[j], axis=0)
        return tuple(states), tuple(sums)

    nstate = alog_ref.shape[0]
    init = (
        tuple(jnp.zeros((nstate, LANES), jnp.float32) for _ in range(tiles)),
        tuple(jnp.zeros((1, LANES), jnp.float32) for _ in range(tiles)),
    )
    states, _ = lax.fori_loop(0, tokens // 8, body, init)
    for j in range(tiles):
        end_ref[:, j * LANES : (j + 1) * LANES] = states[j]


def mix_columns(
    column, span, x_ref, y_ref, cum_ref, alog_ref, start_ref, c_ref, skip_ref, pack_ref, mixer_ref, packed, y_s
):
    tokens = x_ref.shape[0]
    groups, rows, _ = packed.shape
    tiles = span // LANES
    lanes = [pl.ds(pl.multiple_of(column + j * LANES, LANES), LANES) for j in range(tiles)]
    every = pl.ds(pl.multiple_of(column, span), span)
    rates = [-jnp.exp(alog_ref[:, at]) * LOG2E for at in lanes]
    starts = [start_ref[:, at] for at in lanes]

    def body(group, carry):
        base = pl.multiple_of(group * 8, 8)
        partial = [[] for _ in range(tiles)]
        cum8 = cum_ref[pl.ds(base, 8), every]
        for i in range(8):
            ct = c_ref[base + i]
            for j in range(tiles):
                d = cum8[i : i + 1, j * LANES : (j + 1) * LANES]
                partial[j].append(fold_states(ct * (jnp.exp2(rates[j] * d) * starts[j])))
        for j in range(tiles):
            y_s[pl.ds(base, 8), j * LANES : (j + 1) * LANES] = fold(partial[j])
        return carry

    lax.fori_loop(0, tokens // 8, body, 0)
    mixer = (
        y_s[...] + y_ref[:, every] + skip_ref[:, every] * x_ref[:, every].astype(jnp.float32)
    ).astype(jnp.bfloat16)
    mixer_ref[:, every] = mixer
    packed[:, :, every] = (
        jnp.dot(pack_ref[...], mixer, preferred_element_type=jnp.float32)
        .astype(jnp.bfloat16)
        .reshape(groups, rows, span)
    )


def final_kernel(mixer_ref, back_ref, one_ref, two_ref, w_ref, out_ref):
    back = back_ref[...]
    a = jnp.dot(one_ref[...], back, preferred_element_type=jnp.float32)
    b = jnp.dot(two_ref[...], back, preferred_element_type=jnp.float32)
    first = w_ref[:, 0:1]
    second = w_ref[:, 1:2]
    out_ref[...] = (mixer_ref[...].astype(jnp.float32) + (first * a + second * b)).astype(
        jnp.bfloat16
    )


def expert_kernel(
    x_in, y_in, cum_in, alog_in, start_in, c_in, skip_in, pack_in,
    up_ref, up_x_ref, down_ref, back_ref, mixer_ref,
    packed, recv, wu, wd, comb, y_s,
    local_sem, own_sem, z_send, z_recv, r_send, r_recv,
    x_send, x_recv, y_send, y_recv, c_send, c_recv,
):
    groups, rows, channels = packed.shape
    _, shards, depth, hidden_units = wu.shape
    lines = shards // 2
    me, here = lax.axis_index("exp"), lax.axis_index("seq")
    z, h = me // 2, lax.rem(me, 2)
    y, core = here // 2, lax.rem(here, 2)
    partner = {"exp": 2 * z + 1 - h}
    sibling = {"seq": 2 * y + 1 - core}
    mesh_id = pl.DeviceIdType.MESH

    def behind(k):
        return lax.rem(z - k + groups, groups)

    def line_behind(j):
        return lax.rem(y - j + lines, lines)

    def line_peer(j):
        return {"seq": 2 * lax.rem(y + j, lines) + core}

    def remote(src, dst, send, recv_sem, device):
        return pltpu.make_async_remote_copy(
            src_ref=src, dst_ref=dst, send_sem=send, recv_sem=recv_sem,
            device_id=device, device_id_type=mesh_id,
        )

    def wait_into(dst, sem):
        remote(dst, dst, sem, sem, partner).wait_recv()

    barrier = pltpu.get_barrier_semaphore()
    for k in range(1, groups):
        pl.semaphore_signal(
            barrier, inc=1, device_id={"exp": 2 * lax.rem(z + k, groups) + h}, device_id_type=mesh_id
        )
    for j in range(1, lines):
        pl.semaphore_signal(barrier, inc=1, device_id=line_peer(j), device_id_type=mesh_id)
    pl.semaphore_signal(barrier, inc=1, device_id=partner, device_id_type=mesh_id)
    pl.semaphore_signal(barrier, inc=1, device_id=sibling, device_id_type=mesh_id)
    pl.semaphore_wait(barrier, groups + lines)

    def columns(i):
        return pl.ds(pl.multiple_of(i * depth, depth), depth)

    def z_copy(k, i):
        to = lax.rem(z + k, groups)
        return remote(
            packed.at[to, :, columns(i)],
            recv.at[z, :, columns(i)],
            z_send.at[k * shards + i],
            z_recv.at[z * shards + i],
            {"exp": 2 * to + h},
        )

    def r_copy(k, i):
        src = behind(k)
        return remote(
            comb.at[src, :, columns(i)],
            back_ref.at[z, :, columns(i)],
            r_send.at[k * shards + i],
            r_recv.at[z * shards + i],
            {"exp": 2 * src + h},
        )

    def half_of(q):
        return h if q == 0 else 1 - h

    cut = hidden_units // 32 * 16

    def y_copy(kind, j):
        src, dst = (
            (up_ref, wu.at[h, here]),
            (down_ref, wd.at[h, here]),
            (wd.at[1 - h, here, pl.ds(0, cut)], wd.at[1 - h, here, pl.ds(0, cut)]),
        )[kind]
        return remote(src, dst, y_send.at[kind, j], y_recv.at[kind, y], line_peer(j))

    def x_copy(kind, j):
        line = line_behind(j)
        shard = 2 * line + core
        low = wd.at[h, shard, pl.ds(cut, hidden_units - cut)]
        src, dst = ((down_ref, wd.at[h, here]), (wu.at[h, shard], wu.at[h, shard]), (low, low))[kind]
        return remote(src, dst, x_send.at[kind, j], x_recv.at[kind, line], partner)

    def c_copy(w, q, j):
        line = line_behind(j)
        shard = 2 * line + core
        dst = (wu if w == 0 else wd).at[half_of(q), shard]
        src = ((up_ref, up_x_ref.at[1 - h]), (down_ref, dst))[w][q] if j == 0 else dst
        at = (2 * w + half_of(q)) * lines + line
        return remote(src, dst, c_send.at[(2 * w + q) * lines + j], c_recv.at[at], sibling)

    for j in range(1, lines):
        y_copy(0, j).start()
    x_copy(0, 0).start()
    local = [
        pltpu.make_async_copy(up_ref, wu.at[h, here], own_sem.at[0]),
        pltpu.make_async_copy(up_x_ref.at[1 - h], wu.at[1 - h, here], own_sem.at[1]),
        pltpu.make_async_copy(down_ref, wd.at[h, here], own_sem.at[2]),
    ]
    for copy in local:
        copy.start()
    c_copy(0, 0, 0).start()
    c_copy(0, 1, 0).start()
    c_copy(1, 0, 0).start()

    span = y_s.shape[1]

    def mix_step(i, carry):
        def inner(n, inner_carry):
            mix_columns(
                i * depth + n * span, span, x_in, y_in, cum_in, alog_in, start_in, c_in, skip_in,
                pack_in, mixer_ref, packed, y_s,
            )
            return inner_carry

        lax.fori_loop(0, depth // span, inner, 0)
        for k in range(1, groups):
            z_copy(k, i).start()
        return carry

    lax.fori_loop(0, shards, mix_step, 0)

    for j in range(1, lines):
        line = line_behind(j)
        wait_into(wu.at[h, 2 * line + core], y_recv.at[0, line])
        y_copy(1, j).start()
        x_copy(1, j).start()
        c_copy(0, 0, j).start()
    wait_into(wd.at[1 - h, here], x_recv.at[0, y])
    for j in range(1, lines):
        y_copy(2, j).start()
    c_copy(1, 1, 0).start()
    for j in range(1, lines):
        line = line_behind(j)
        shard = 2 * line + core
        wait_into(wd.at[h, shard], y_recv.at[1, line])
        x_copy(2, j).start()
        c_copy(1, 0, j).start()
    for j in range(1, lines):
        line = line_behind(j)
        shard = 2 * line + core
        wait_into(wu.at[1 - h, shard], x_recv.at[1, line])
        c_copy(0, 1, j).start()
    for j in range(1, lines):
        line = line_behind(j)
        shard = 2 * line + core
        wait_into(wd.at[1 - h, shard, pl.ds(0, cut)], y_recv.at[2, line])
        wait_into(wd.at[1 - h, shard, pl.ds(cut, hidden_units - cut)], x_recv.at[2, line])
        c_copy(1, 1, j).start()
    for copy in local:
        copy.wait()
    for w in range(2):
        for half in range(2):
            for j in range(lines):
                line = line_behind(j)
                wait_into(
                    (wu if w == 0 else wd).at[half, 2 * line + 1 - core],
                    c_recv.at[(2 * w + half) * lines + line],
                )

    def compute(first, second):
        sources = [behind(first), behind(second)]
        zero = jnp.zeros((2 * rows, hidden_units), jnp.float32)

        def up_step(i, acc):
            cols = columns(i)
            for k, src in zip((first, second), sources):
                if k:
                    wait_into(recv.at[src, :, cols], z_recv.at[src * shards + i])
            block = jnp.concatenate(
                [
                    (recv if k else packed)[src, :, cols]
                    for k, src in zip((first, second), sources)
                ],
                axis=0,
            )
            return tuple(
                acc[n] + jnp.dot(block, wu[n, i], preferred_element_type=jnp.float32)
                for n in range(2)
            )

        pre = lax.fori_loop(0, shards, up_step, (zero, zero))
        hidden = [(p / (1.0 + jnp.exp(-p))).astype(jnp.bfloat16) for p in pre]

        def down_step(i, carry):
            cols = columns(i)
            total = sum(
                jnp.dot(hidden[n], wd[n, i], preferred_element_type=jnp.float32)
                .astype(jnp.bfloat16)
                .astype(jnp.float32)
                for n in range(2)
            ).astype(jnp.bfloat16)
            for n, src in enumerate(sources):
                comb[src, :, cols] = total[n * rows : (n + 1) * rows]
            for k in (first, second):
                if k:
                    r_copy(k, i).start()
            return carry

        lax.fori_loop(0, shards, down_step, 0)
    order = list(range(1, groups)) + [0]
    for k in range(0, groups, 2):
        compute(order[k], order[k + 1])
    keep = pltpu.make_async_copy(comb.at[z], back_ref.at[z], local_sem.at[0])
    keep.start()
    keep.wait()
    for k in range(1, groups):
        src = behind(k)

        def finish(i, carry):
            wait_into(back_ref.at[src, :, columns(i)], r_recv.at[src * shards + i])
            z_copy(k, i).wait_send()
            r_copy(k, i).wait_send()
            return carry

        lax.fori_loop(0, shards, finish, 0)
    x_copy(0, 0).wait_send()
    for j in range(1, lines):
        for kind in range(3):
            y_copy(kind, j).wait_send()
        x_copy(1, j).wait_send()
        x_copy(2, j).wait_send()
    for w in range(2):
        for q in range(2):
            for j in range(lines):
                c_copy(w, q, j).wait_send()


def run_experts(mix_inputs, groups, span, w_up, up_x, w_down):
    tokens, channels = mix_inputs[0].shape
    rows = mix_inputs[-1].shape[0] // groups
    depth, hidden_units = w_up.shape
    shards = channels // depth
    lines = shards // 2
    span = min(span, depth)
    dma = pltpu.SemaphoreType.DMA
    any_spec = pl.BlockSpec(memory_space=pl.ANY)
    vmem_spec = pl.BlockSpec(memory_space=pltpu.VMEM)
    bf16 = jnp.bfloat16
    return pl.pallas_call(
        expert_kernel,
        in_specs=[vmem_spec] * len(mix_inputs) + [any_spec] * 3,
        out_specs=[any_spec, vmem_spec],
        out_shape=[
            jax.ShapeDtypeStruct((groups, rows, channels), bf16),
            jax.ShapeDtypeStruct((tokens, channels), bf16),
        ],
        scratch_shapes=[
            pltpu.VMEM((groups, rows, channels), bf16),
            pltpu.VMEM((groups, rows, channels), bf16),
            pltpu.VMEM((2, shards, depth, hidden_units), bf16),
            pltpu.VMEM((2, shards, hidden_units, depth), bf16),
            pltpu.VMEM((groups, rows, channels), bf16),
            pltpu.VMEM((tokens, span), jnp.float32),
            dma((1,)),
            dma((3,)),
        ]
        + [dma((groups * shards,)) for _ in range(4)]
        + [dma((3, lines)) for _ in range(4)]
        + [dma((4 * lines,)), dma((4 * lines,))],
        compiler_params=pltpu.CompilerParams(
            collective_id=0, has_side_effects=True, vmem_limit_bytes=58 * 1024 * 1024
        ),
        name="experts",
    )(*mix_inputs, w_up, up_x, w_down)


def whole_spec(*shape):
    return pl.BlockSpec(shape, lambda i: (0,) * len(shape))


def vector_cost(updates):
    return pl.CostEstimate(flops=2048 * updates, bytes_accessed=6 * updates, transcendentals=updates)


def run_scan(x, dt, w_dt, bias, a_log, b_wide, c_wide, span):
    tokens, channels = x.shape
    rank, nstate = dt.shape[1], a_log.shape[0]
    cols = lambda rows: pl.BlockSpec((rows, span), lambda i: (0, i))
    return pl.pallas_call(
        scan_kernel,
        grid=(channels // span,),
        in_specs=[
            cols(tokens),
            whole_spec(tokens, rank),
            cols(rank),
            cols(1),
            cols(nstate),
            whole_spec(tokens, nstate, LANES),
            whole_spec(tokens, nstate, LANES),
        ],
        out_specs=[cols(tokens), cols(tokens), cols(nstate)],
        out_shape=[
            jax.ShapeDtypeStruct((tokens, channels), jnp.float32),
            jax.ShapeDtypeStruct((tokens, channels), jnp.float32),
            jax.ShapeDtypeStruct((nstate, channels), jnp.float32),
        ],
        scratch_shapes=[
            pltpu.VMEM((tokens, span), jnp.float32),
            pltpu.VMEM((tokens, span), jnp.float32),
        ],
        compiler_params=pltpu.CompilerParams(vmem_limit_bytes=32 * 1024 * 1024),
        cost_estimate=vector_cost(tokens * nstate * channels),
        name="scan_local",
    )(x, dt, w_dt, bias[None], a_log, b_wide, c_wide)


def run_final(mixer, back, one, two, weights, span):
    tokens, channels = mixer.shape
    slots = back.shape[0]
    cols = lambda rows: pl.BlockSpec((rows, span), lambda i: (0, i))
    return pl.pallas_call(
        final_kernel,
        grid=(channels // span,),
        in_specs=[
            cols(tokens),
            cols(slots),
            whole_spec(tokens, slots),
            whole_spec(tokens, slots),
            whole_spec(tokens, 2),
        ],
        out_specs=cols(tokens),
        out_shape=jax.ShapeDtypeStruct((tokens, channels), jnp.bfloat16),
        compiler_params=pltpu.CompilerParams(vmem_limit_bytes=32 * 1024 * 1024),
        name="final_sum",
    )(mixer, back, one, two, weights)


def shift(value, by):
    count = lax.axis_size("seq")
    return lax.ppermute(value, "seq", [(i, i + by) for i in range(count - by)])


def carry_in(a_neg, total, end_state):
    count = lax.axis_size("seq")
    both = jnp.concatenate([end_state, total], axis=0)
    start = jnp.zeros_like(end_state)
    between = jnp.zeros_like(total)
    if count <= 4:
        arrived = [shift(both, by) for by in range(1, count)]
        for item in arrived:
            start = start + jnp.exp(a_neg * between) * item[:-1]
            between = between + item[-1:]
        return start

    def relay(index, incoming):
        return shift(jnp.exp(a_neg * total) * incoming + end_state, 1)

    return lax.fori_loop(0, count - 1, relay, start)


def routing(picks, groups, rows):
    tokens = picks.shape[0]
    flat = picks.reshape(-1)
    onehot = (flat[:, None] == jnp.arange(groups, dtype=jnp.int32)[None, :]).astype(jnp.float32)
    steps = jnp.arange(2 * tokens, dtype=jnp.int32)
    earlier = (steps[:, None] > steps[None, :]).astype(jnp.float32)
    before = jnp.dot(earlier, onehot, preferred_element_type=jnp.float32)
    position = jnp.sum(onehot * before, axis=1).astype(jnp.int32)
    place = (flat * rows + position).reshape(tokens, 2)
    slots = jnp.arange(groups * rows, dtype=jnp.int32)
    one = (place[:, 0:1] == slots[None, :]).astype(jnp.bfloat16)
    two = (place[:, 1:2] == slots[None, :]).astype(jnp.bfloat16)
    pack = (
        (place[:, 0][None, :] == slots[:, None]) | (place[:, 1][None, :] == slots[:, None])
    ).astype(jnp.bfloat16)
    return one, two, pack


def per_device(
    x_act, dt_low, b_c, w_dt, dt_bias, a_log, d_skip, w_router, expert_ids, w_up, w_down
):
    x, dt = x_act[0], dt_low[0]
    tokens, channels = x.shape
    nstate = a_log.shape[0]
    groups = w_router.shape[0]
    owners = lax.axis_size("exp")
    capacity = 5 * tokens // owners
    rows = -(-capacity // 16) * 16
    span = 512
    picks = expert_ids[0]
    pairs = [[i, i + 1] for i in range(0, owners, 2)]
    up_x = lax.all_gather(w_up[0], "exp", axis_index_groups=pairs)
    one, two, pack = routing(picks, groups, rows)
    wide = jnp.broadcast_to(b_c[0][:, :, None], b_c.shape[1:] + (LANES,))
    b_wide, c_wide = wide[:, :nstate], wide[:, nstate:]
    y, cum, end_state = run_scan(x, dt, w_dt, dt_bias, a_log, b_wide, c_wide, span)
    start = carry_in(-jnp.exp(a_log), cum[-1:], end_state)
    mix_inputs = (x, y, cum, a_log, start, c_wide, d_skip[None], pack)
    back, mixer = run_experts(mix_inputs, groups, span, w_up[0], up_x, w_down[0])
    logits = jnp.dot(mixer, w_router.T, preferred_element_type=jnp.float32)
    ids = jnp.arange(groups, dtype=jnp.int32)
    gap = jnp.sum(
        jnp.where(picks[:, 0:1] == ids, logits, 0.0) - jnp.where(picks[:, 1:2] == ids, logits, 0.0),
        axis=1,
        keepdims=True,
    )
    first = jax.nn.sigmoid(gap)
    weights = jnp.concatenate([first, 1.0 - first], axis=1)

    back = back.reshape(-1, channels)
    return run_final(mixer, back, one, two, weights, span)[None]


def solution(mesh):
    in_specs = (
        P("exp", "seq", None),
        P("exp", "seq", None),
        P("exp", "seq", None),
        P(),
        P(),
        P(),
        P(),
        P(),
        P("exp", "seq", None),
        P("exp", "seq", None),
        P("exp", None, "seq"),
    )
    out_specs = P("exp", "seq", None)
    return jax.shard_map(
        per_device, mesh=mesh, in_specs=in_specs, out_specs=out_specs, check_vma=False
    )
```
